128 devices in a mesh: rep: 8 (over z_hi, y), shard: 16 (over z_lo, x, core).
Axes of the slice: x: 4, y: 4, z: 4 (z_hi: 2, z_lo: 2; z = z_hi * 2 + z_lo), core: 2. Of those that a mesh axis runs over, the one named last changes fastest.
Arguments:
- residuals: bfloat16 [32, 1024, 4, 1024], P('shard', 'rep'), may hold values from -6 to 6
- lengths: int32 [32], P('shard'), may hold values from 256 to 1024, as said below
- w_query: bfloat16 [1024, 2048], P('shard'), may hold values from -0.1875 to 0.1875
- w_key: bfloat16 [1024, 1024], P('shard'), may hold values from -0.1875 to 0.1875
- w_value: bfloat16 [1024, 1024], P('shard'), may hold values from -0.1875 to 0.1875
- w_out: bfloat16 [2048, 1024], P('shard'), may hold values from -1 to 1
- w_gate: bfloat16 [1024, 3072], P('shard'), may hold values from -0.1875 to 0.1875
- w_up: bfloat16 [1024, 3072], P('shard'), may hold values from -0.1875 to 0.1875
- w_down: bfloat16 [3072, 1024], P('shard'), may hold values from -0.109375 to 0.109375
- attn_gain: float32 [1024], replicated, may hold values from 0.25 to 1.75
- mlp_gain: float32 [1024], replicated, may hold values from 0.25 to 1.75
- query_gain: float32 [128], replicated, may hold values from 0.25 to 1.75
- key_gain: float32 [128], replicated, may hold values from 0.25 to 1.75
- hyper_weight: float32 [2, 6, 1024], replicated, may hold values from -0.09375 to 0.09375
- hyper_static: float32 [2, 4, 6], replicated, may hold values from -3 to 3
- cotangent: bfloat16 [32, 1024, 4, 1024], P('shard', 'rep'), may hold values from -6 to 6
Outputs:
- out_residuals: bfloat16 [32, 1024, 4, 1024], P('shard', 'rep')
- grad_residuals: float32 [32, 1024, 4, 1024], P('shard', 'rep')
- grad_query: float32 [1024, 2048], P('shard')
- grad_key: float32 [1024, 1024], P('shard')
- grad_value: float32 [1024, 1024], P('shard')
- grad_out: float32 [2048, 1024], P('shard')
- grad_gate: float32 [1024, 3072], P('shard')
- grad_up: float32 [1024, 3072], P('shard')
- grad_down: float32 [3072, 1024], P('shard')
- grad_attn_gain: float32 [1024], replicated
- grad_mlp_gain: float32 [1024], replicated
- grad_query_gain: float32 [128], replicated
- grad_key_gain: float32 [128], replicated
- grad_hyper_weight: float32 [2, 6, 1024], replicated
- grad_hyper_static: float32 [2, 4, 6], replicated
The draws below stay inside these ranges and needn't reach their ends.
Inputs may be any that keep to these rules, and one draw needn't show every extreme that they name: Positions 0 to lengths[b] - 1 of sequence b are its tokens; the rest is padding.
All inputs are finite; a program needn't handle non-finite values.
Results may differ from the reference program's by a relative error of at most 0.025.
Values may be sent and summed in bfloat16 or wider, within the bound.
No kernel may reach another device: no remote copies, remote signals or barrier semaphores. Data moves between devices by JAX's collectives and lax.ppermute only.
A program may use at most 256 MiB of HBM per device.

```python
import jax
import jax.numpy as jnp
from jax import lax

D = 1024
HEADS = 16
KV_HEADS = 8
HEAD_DIM = 128
FF = 3072
LANES = 4
QD = 2048
KVD = 1024
HC = 6
SEQ_LEN = 1024
SEQS = 32


def draw_lengths(key, part):
    key = jax.random.fold_in(key, 11)
    key_full, key_other = jax.random.split(key)
    pair_count = SEQS // 2
    full_side = jax.random.randint(key_full, (pair_count,), 0, 2)
    other_len = jax.random.randint(key_other, (pair_count,), SEQ_LEN // 4, SEQ_LEN + 1)
    left_len = jnp.where(full_side == 0, SEQ_LEN, other_len)
    right_len = jnp.where(full_side == 0, other_len, SEQ_LEN)
    return jnp.stack([left_len, right_len], axis=1).reshape(SEQS).astype(jnp.int32)


def steps_of(key, dims, cuts, least, high):
    factor_of, own = 1.0, jax.random.fold_in(key, 6)
    for position, blocks in cuts:
        heights = jnp.exp(jax.random.uniform(jax.random.fold_in(own, position), (blocks,), jnp.float32, least / len(cuts), high / len(cuts)))
        factor_of = factor_of * jnp.repeat(heights, dims[position] // blocks).reshape([-1 if axis == position else 1 for axis in range(len(dims))])
    return factor_of


def bell_draw(key, dims, deviation, reach, pieces=(), kind=jnp.bfloat16):
    level = steps_of(key, dims, pieces, -0.22, 0.18) if pieces else 1.0
    array = jax.random.normal(key, dims, jnp.float32) * deviation * level
    return jnp.minimum(jnp.maximum(array, -reach), reach).astype(kind)


def setup_inputs(seed: int = 0) -> dict:
    streams_of = jax.random.split(jax.random.key(seed), 17)
    residuals = bell_draw(streams_of[0], (SEQS, SEQ_LEN, LANES, D), 1.0, 6.0, ((0, 16), (1, 8)))
    lengths = draw_lengths(jax.random.fold_in(streams_of[16], 71), 0)
    w_query = bell_draw(streams_of[2], (D, QD), D ** -0.5, 0.1875, ((0, 16),))
    w_key = bell_draw(streams_of[3], (D, KVD), D ** -0.5, 0.1875, ((0, 16),))
    w_value = bell_draw(streams_of[4], (D, KVD), D ** -0.5, 0.1875, ((0, 16),))
    w_out = bell_draw(streams_of[5], (QD, D), (max(1, 16 * QD // SEQ_LEN)) ** -0.5, 1.0, ((0, 16),))
    w_gate = bell_draw(streams_of[6], (D, FF), D ** -0.5, 0.1875, ((0, 16),))
    w_up = bell_draw(streams_of[7], (D, FF), D ** -0.5, 0.1875, ((0, 16),))
    w_down = bell_draw(streams_of[8], (FF, D), FF ** -0.5, 0.109375, ((0, 16),))
    attn_gain = jnp.clip(1.0 + 0.15 * jax.random.normal(streams_of[9], (D,), jnp.float32), 0.25, 1.75)
    mlp_gain = jnp.clip(1.0 + 0.15 * jax.random.normal(streams_of[10], (D,), jnp.float32), 0.25, 1.75)
    query_gain = jnp.clip(1.0 + 0.15 * jax.random.normal(streams_of[11], (HEAD_DIM,), jnp.float32), 0.25, 1.75)
    key_gain = jnp.clip(1.0 + 0.15 * jax.random.normal(streams_of[12], (HEAD_DIM,), jnp.float32), 0.25, 1.75)
    hyper_weight = bell_draw(streams_of[13], (2, HC, D), (4 * D) ** -0.5, 0.09375, (), jnp.float32)
    hyper_static = bell_draw(streams_of[14], (2, LANES, HC), 0.5, 3.0, (), jnp.float32)
    cotangent = bell_draw(streams_of[15], (SEQS, SEQ_LEN, LANES, D), 1.0, 6.0, ((0, 16), (1, 8)))
    return {"residuals": residuals, "lengths": lengths, "w_query": w_query, "w_key": w_key, "w_value": w_value, "w_out": w_out, "w_gate": w_gate, "w_up": w_up, "w_down": w_down, "attn_gain": attn_gain, "mlp_gain": mlp_gain, "query_gain": query_gain, "key_gain": key_gain, "hyper_weight": hyper_weight, "hyper_static": hyper_static, "cotangent": cotangent}


@jax.custom_vjp
def low(v):
    return lax.optimization_barrier(v.astype(jnp.bfloat16)).astype(jnp.float32)

@jax.custom_vjp
def low_back(v):
    return v

def low_keep(v):
    return (low(v), None)

def low_pass(kept, grad):
    return (grad,)

def back_keep(v):
    return (v, None)

def back_low(kept, grad):
    return (low(grad),)
low.defvjp(low_keep, low_pass)
low_back.defvjp(back_keep, back_low)
EPSILON = 1e-06
ROTARY_BASE = 1000000.0
MASKED = -1e+30

def matmul(left_op, right_op):
    return jnp.dot(left_op, right_op, precision=lax.Precision.HIGHEST)

def rms_scale(values, gain_vec):
    return values * lax.rsqrt(lax.optimization_barrier(jnp.mean(values * values, axis=-1, keepdims=True)) + EPSILON) * gain_vec

def rotary_tables(positions, head_dim):
    half_dim = head_dim // 2
    inverse = ROTARY_BASE ** (-jnp.arange(half_dim, dtype=jnp.float32) * 2.0 / head_dim)
    angles = positions.astype(jnp.float32)[:, None] * inverse[None, :]
    angles = jnp.concatenate([angles, angles], axis=1)
    return (jnp.cos(angles), jnp.sin(angles))

def head_rotary(values, gain_vec, cos_tab, sin_tab, head_count):
    row_count = values.shape[0]
    shaped = rms_scale(values.reshape(row_count, head_count, -1), gain_vec)
    half_dim = shaped.shape[-1] // 2
    turned = jnp.concatenate([-shaped[..., half_dim:], shaped[..., :half_dim]], axis=-1)
    return (shaped * cos_tab[:, None, :] + turned * sin_tab[:, None, :]).reshape(row_count, -1)

def lane_inputs(lanes, mixing, static, gain_vec):
    lane_count = lanes.shape[1]
    normed = lanes * lax.rsqrt(lax.optimization_barrier(jnp.mean(lanes * lanes, axis=-1, keepdims=True)) + EPSILON)
    coeffs = jnp.tanh(jnp.einsum('tsd,kd->tsk', normed, mixing, precision=lax.Precision.HIGHEST)) + static
    joined = jnp.einsum('ts,tsd->td', coeffs[:, :, 0], lanes, precision=lax.Precision.HIGHEST)
    return (rms_scale(joined, gain_vec), coeffs[:, :, 1:1 + lane_count], coeffs[:, :, 1 + lane_count])

def lane_outputs(lanes, mix_coef, out_coef, branch):
    return jnp.einsum('tij,tid->tjd', mix_coef, lanes, precision=lax.Precision.HIGHEST) + out_coef[:, :, None] * branch[:, None, :]

def attention(query_act, key_act, value_act, length):
    row_count = query_act.shape[0]
    grouped = query_act.reshape(row_count, KV_HEADS, HEADS // KV_HEADS, HEAD_DIM)
    key_heads = key_act.reshape(row_count, KV_HEADS, HEAD_DIM)
    value_heads = value_act.reshape(row_count, KV_HEADS, HEAD_DIM)
    scores = low_back(jnp.einsum('qkgd,pkd->kgqp', grouped, key_heads, precision=lax.Precision.HIGHEST) * HEAD_DIM ** (-0.5))
    places = jnp.arange(row_count)
    allowed = (places[None, :] <= places[:, None]) & (places[None, :] < length)
    scores = jnp.where(allowed, scores, MASKED)
    row_max = lax.optimization_barrier(jnp.max(scores, axis=-1, keepdims=True))
    weights = jnp.exp(scores - row_max)
    weights = weights / lax.optimization_barrier(jnp.sum(weights, axis=-1, keepdims=True))
    attended = jnp.einsum('kgqp,pkd->qkgd', low(weights), value_heads, precision=lax.Precision.HIGHEST)
    return attended.reshape(row_count, -1)

def layer(params, lanes, length):
    w_query, w_key, w_value, w_out, w_gate, w_up, w_down, attn_gain, mlp_gain, query_gain, key_gain, hyper_weight, hyper_static = params
    places = jnp.arange(lanes.shape[0])
    cos_tab, sin_tab = rotary_tables(places, HEAD_DIM)
    normed, mix_coef, out_coef = lane_inputs(lanes, hyper_weight[0], hyper_static[0], attn_gain)
    normed = low(normed)
    query_act = low_back(matmul(normed, w_query))
    key_act = low_back(matmul(normed, w_key))
    value_act = low(low_back(matmul(normed, w_value)))
    query_act = low(head_rotary(query_act, query_gain, cos_tab, sin_tab, HEADS))
    key_act = low(head_rotary(key_act, key_gain, cos_tab, sin_tab, KV_HEADS))
    attended = low(low_back(attention(query_act, key_act, value_act, length)))
    branch = low_back(matmul(attended, w_out))
    lanes = lane_outputs(lanes, mix_coef, out_coef, branch)
    normed, mix_coef, out_coef = lane_inputs(lanes, hyper_weight[1], hyper_static[1], mlp_gain)
    normed = low(normed)
    gate_act = low_back(matmul(normed, w_gate))
    upward = low_back(matmul(normed, w_up))
    hidden = low(jax.nn.silu(gate_act) * upward)
    branch = low_back(matmul(hidden, w_down))
    return lane_outputs(lanes, mix_coef, out_coef, branch)

def reference(residuals, lengths, w_query, w_key, w_value, w_out, w_gate, w_up, w_down, attn_gain, mlp_gain, query_gain, key_gain, hyper_weight, hyper_static, cotangent):
    params = tuple((item.astype(jnp.float32) for item in (w_query, w_key, w_value, w_out, w_gate, w_up, w_down, attn_gain, mlp_gain, query_gain, key_gain, hyper_weight, hyper_static)))

    def one_sequence(totals, inputs):
        seq_block, length, tangent = inputs
        places = jnp.arange(SEQ_LEN)
        valid_rows = (places < length).astype(jnp.float32)
        result, pullback = jax.vjp(lambda weights, values: layer(weights, values, length), params, seq_block.astype(jnp.float32))
        weight_grads, lane_grads = pullback(tangent.astype(jnp.float32) * valid_rows[:, None, None])
        totals = jax.tree.map(jnp.add, totals, weight_grads)
        return (totals, (result.astype(jnp.bfloat16), lane_grads))
    zero_grads = jax.tree.map(jnp.zeros_like, params)
    totals, (new_lanes, lane_grads) = lax.scan(one_sequence, zero_grads, (residuals, lengths, cotangent))
    return (new_lanes, lane_grads, totals[0], totals[1], totals[2], totals[3], totals[4], totals[5], totals[6], totals[7], totals[8], totals[9], totals[10], totals[11], totals[12])
```

```python
from functools import partial

import jax
import jax.numpy as jnp
from jax import lax
from jax.experimental import pallas as pl
from jax.experimental.pallas import tpu as pltpu
from jax.sharding import PartitionSpec as P

EPSILON = 1e-06
ROTARY_BASE = 1000000.0
MASKED = -1e30
LANES = 4
SPAN = 32
PACK = 128
NT = (((1,), (1,)), ((), ()))
NN = (((1,), (0,)), ((), ()))
TN = (((0,), (0,)), ((), ()))
F32 = jnp.float32
BF16 = jnp.bfloat16
VMEM_LIMIT = 60 * 1024 * 1024
CHUNK = 64


def mm(a, b, dims=NN):
    return lax.dot_general(a, b, dims, preferred_element_type=F32)


def params(limit=VMEM_LIMIT):
    return pltpu.CompilerParams(vmem_limit_bytes=limit)


def lane_mask(column):
    spot = lax.broadcasted_iota(jnp.int32, (1, PACK), 1)
    return (spot == column).astype(F32)


def group_mask(lane):
    spot = lax.broadcasted_iota(jnp.int32, (1, PACK), 1)
    return (spot // 8 == lane).astype(F32)


def row_sum(values):
    return jnp.sum(values, axis=1, keepdims=True)


def col(coefs, index):
    return coefs[:, index : index + 1]


def rsqrt_mean(values):
    return lax.rsqrt(row_sum(values * values) * (1.0 / values.shape[1]) + EPSILON)


def lanes_of(ref, rows, width):
    return [ref[rows, i * width : (i + 1) * width].astype(F32) for i in range(LANES)]


def scale_pack(lanes):
    out = 0.0
    for i, h in enumerate(lanes):
        out = out + rsqrt_mean(h) * group_mask(i)
    return out


def mixed(coefs, lanes, j):
    out = col(coefs, 1 + j) * lanes[0]
    for i in range(1, LANES):
        out = out + col(coefs, 8 * i + 1 + j) * lanes[i]
    return out


def unmixed(coefs, grads, i):
    out = col(coefs, 8 * i + 1) * grads[0]
    for j in range(1, LANES):
        out = out + col(coefs, 8 * i + 1 + j) * grads[j]
    return out


def joined(coefs, lanes):
    out = col(coefs, 0) * lanes[0]
    for i in range(1, LANES):
        out = out + col(coefs, 8 * i) * lanes[i]
    return out


def branch_grad(coefs, grads):
    out = col(coefs, 5) * grads[0]
    for j in range(1, LANES):
        out = out + col(coefs, 8 * j + 5) * grads[j]
    return out


def mix_grads(lanes, grads, branch):
    out = 0.0
    for j in range(LANES):
        for i in range(LANES):
            out = out + row_sum(lanes[i] * grads[j]) * lane_mask(8 * i + 1 + j)
        out = out + row_sum(branch * grads[j]) * lane_mask(8 * j + 5)
    return out


def fold_low(raw):
    return raw + (pltpu.roll(raw, PACK - 2 * SPAN, 1) + pltpu.roll(raw, PACK - 3 * SPAN, 1))


def two_parts(values):
    high = values.astype(BF16)
    return high, (values - high.astype(F32)).astype(BF16)


def split_pack(values):
    high = values.astype(BF16).astype(F32)
    return (high + pltpu.roll(values - high, SPAN, 1) + pltpu.roll(high, 2 * SPAN, 1)).astype(BF16)


def hyper_rows(dtr_pack, lane_low, i):
    full = mm(dtr_pack, lane_low, TN)
    return full[8 * i : 8 * i + 8] + full[SPAN + 8 * i : SPAN + 8 * i + 8]


def fold8(values):
    rows = values.shape[0]
    out = values[0:8]
    for at in range(8, rows, 8):
        out = out + values[at : at + 8]
    return out


def pack_kernel(w_ref, out_ref):
    layers, count, width = w_ref.shape
    blank = jnp.zeros((8, width), F32)
    for layer in range(layers):
        w = jnp.concatenate([w_ref[layer], jnp.zeros((8 - count, width), F32)], axis=0)
        high = w.astype(BF16).astype(F32)
        for i in range(LANES):
            pieces = [blank] * (PACK // 8)
            pieces[i] = pieces[SPAN // 8 + i] = high
            pieces[2 * SPAN // 8 + i] = low = (w - high).astype(BF16).astype(F32)
            pieces[3 * SPAN // 8 + i] = (w - high) - low
            out_ref[layer, i] = jnp.concatenate(pieces, axis=0).astype(BF16)


def pack(hyper_weight):
    layers, _, width = hyper_weight.shape
    vm = pl.BlockSpec(memory_space=pltpu.VMEM)
    return pl.pallas_call(
        pack_kernel,
        in_specs=[vm],
        out_specs=vm,
        out_shape=jax.ShapeDtypeStruct((layers, LANES, PACK, width), BF16),
        compiler_params=params(),
        name="pack_hyper_weights",
    )(hyper_weight)


def pre_kernel(h_ref, w_ref, static_ref, gain_ref, x_ref, coef_ref, z_ref, raw_ref):
    rows, width = x_ref.shape
    acc = 0.0
    for i in range(LANES):
        acc = acc + mm(h_ref[:, i * width : (i + 1) * width], w_ref[i], NT)
    raw_ref[...] = acc

    @pl.loop(0, rows // CHUNK)
    def _(step):
        rs = pl.ds(pl.multiple_of(step * CHUNK, CHUNK), CHUNK)
        lanes = lanes_of(h_ref, rs, width)
        z = fold_low(raw_ref[rs, :]) * scale_pack(lanes)
        coefs = jnp.tanh(z) + static_ref[...]
        x = joined(coefs, lanes)
        x_ref[rs, :] = (x * rsqrt_mean(x) * gain_ref[...]).astype(BF16)
        coef_ref[rs, :] = coefs
        z_ref[rs, :] = z


def pre(h, wrow, static, gain):
    rows, width4 = h.shape
    width = width4 // LANES
    block = rows // 2
    return pl.pallas_call(
        pre_kernel,
        grid=(2,),
        in_specs=[
            pl.BlockSpec((block, width4), lambda g: (g, 0)),
            pl.BlockSpec((LANES, PACK, width), lambda g: (0, 0, 0)),
            pl.BlockSpec((1, PACK), lambda g: (0, 0)),
            pl.BlockSpec((1, width), lambda g: (0, 0)),
        ],
        out_specs=[
            pl.BlockSpec((block, width), lambda g: (g, 0)),
            pl.BlockSpec((block, PACK), lambda g: (g, 0)),
            pl.BlockSpec((block, PACK), lambda g: (g, 0)),
        ],
        out_shape=[
            jax.ShapeDtypeStruct((rows, width), BF16),
            jax.ShapeDtypeStruct((rows, PACK), F32),
            jax.ShapeDtypeStruct((rows, PACK), F32),
        ],
        scratch_shapes=[pltpu.VMEM((block, PACK), F32)],
        compiler_params=params(),
        name="lane_in_zero",
    )(h, wrow, static, gain)


def rotate(u, gain, cos, sin_signed):
    half = u.shape[1] // 2
    m = u * rsqrt_mean(u) * gain
    return m * cos + pltpu.roll(m, half, 1) * sin_signed


def qkv_kernel(x_ref, w_ref, qg_ref, kg_ref, cos_ref, sin_ref, send_ref, keep_ref):
    hd = qg_ref.shape[1]
    rows = x_ref.shape[0]
    half = x_ref.shape[1] // 2
    u = 0.0
    for z in range(2):
        w = w_ref[:, z].reshape(half, 4 * hd)
        u = u + mm(x_ref[:, z * half : (z + 1) * half], w)
    half_rows = rows // 2
    for part in range(2):
        rs = slice(part * half_rows, (part + 1) * half_rows)
        cos, sin = cos_ref[...], sin_ref[...]
        for k in range(3):
            cs = slice(k * hd, (k + 1) * hd)
            piece = u[rs, cs]
            keep_ref[0, rs, cs] = piece
            gain = qg_ref[...] if k < 2 else kg_ref[...]
            send_ref[0, rs, cs] = rotate(piece, gain, cos, sin).astype(BF16)
        send_ref[0, rs, 3 * hd :] = u[rs, 3 * hd :].astype(BF16)


def qkv(x, w_grouped, q_gain, k_gain, cos, sin_signed):
    rows, width = x.shape
    hd = q_gain.shape[1]
    groups = w_grouped.shape[3] // (4 * hd)
    return pl.pallas_call(
        qkv_kernel,
        grid=(groups,),
        in_specs=[
            pl.BlockSpec((rows, width), lambda g: (0, 0)),
            pl.BlockSpec(w_grouped.shape[:3] + (4 * hd,), lambda g: (0, 0, 0, g)),
            pl.BlockSpec((1, hd), lambda g: (0, 0)),
            pl.BlockSpec((1, hd), lambda g: (0, 0)),
            pl.BlockSpec(cos.shape, lambda g: (0, 0)),
            pl.BlockSpec(cos.shape, lambda g: (0, 0)),
        ],
        out_specs=[
            pl.BlockSpec((1, rows, 4 * hd), lambda g: (g, 0, 0)),
            pl.BlockSpec((1, rows, 3 * hd), lambda g: (g, 0, 0)),
        ],
        out_shape=[
            jax.ShapeDtypeStruct((groups, rows, 4 * hd), BF16),
            jax.ShapeDtypeStruct((groups, rows, 3 * hd), F32),
        ],
        compiler_params=params(),
        name="qkv_rotary",
    )(x, w_grouped, q_gain, k_gain, cos, sin_signed)


QB = 256


def allowed_at(i, kb, length, block):
    row = lax.broadcasted_iota(jnp.int32, (2 * block, block), 0)
    row = jnp.where(row >= block, row - block, row) + i * block
    key = lax.broadcasted_iota(jnp.int32, (2 * block, block), 1) + kb * block
    return (key <= row) & (key < length)


def two_heads(ref, i, per, hd, at=0):
    first = ref[pl.ds(i * per, per), 0, :, at * hd : (at + 1) * hd]
    second = ref[pl.ds(i * per, per), 0, :, (at + 1) * hd : (at + 2) * hd]
    return jnp.concatenate([first.reshape(-1, hd), second.reshape(-1, hd)], axis=0)


def one_head(ref, i, per, hd, at):
    return ref[pl.ds(i * per, per), 0, :, at * hd : (at + 1) * hd].reshape(-1, hd)


def attend_kernel(len_ref, x_ref, o_ref, lse_ref, s_ref):
    sources, _, places, width = x_ref.shape
    hd = width // 4
    per = QB // places
    scale = hd**-0.5
    length = len_ref[pl.program_id(0)]

    @pl.loop(0, sources * places // QB)
    def _(i):
        q = two_heads(x_ref, i, per, hd)

        def score(kb, top):
            s = mm(q, one_head(x_ref, kb, per, hd, 2), NT) * scale
            s = jnp.where(allowed_at(i, kb, length, QB), s, MASKED)
            s_ref[kb] = s
            for at in range(0, QB, 128):
                top = jnp.maximum(top, s[:, at : at + 128])
            return top

        top = lax.fori_loop(0, i + 1, score, jnp.full((2 * QB, 128), MASKED, F32))
        top = jnp.max(top, axis=1, keepdims=True)

        def weigh(kb, total):
            p = jnp.exp(s_ref[kb] - top)
            s_ref[kb] = p
            for at in range(0, QB, 128):
                total = total + p[:, at : at + 128]
            return total

        total = row_sum(lax.fori_loop(0, i + 1, weigh, jnp.zeros((2 * QB, 128), F32)))
        inverse = 1.0 / total

        def gather(kb, acc):
            p = (s_ref[kb] * inverse).astype(BF16)
            return acc + mm(p, one_head(x_ref, kb, per, hd, 3))

        o = lax.fori_loop(0, i + 1, gather, jnp.zeros((2 * QB, hd), F32)).astype(BF16)
        lse_ref[0, i] = jnp.broadcast_to(top + jnp.log(total), (2 * QB, 128))
        o_ref[pl.ds(i * per, per), 0, :, 0:hd] = o[:QB].reshape(per, places, hd)
        o_ref[pl.ds(i * per, per), 0, :, hd:] = o[QB:].reshape(per, places, hd)


def attend(lengths, x):
    sources, pairs, places, width = x.shape
    hd = width // 4
    blocks = sources * places // QB
    return pl.pallas_call(
        attend_kernel,
        grid=(pairs,),
        in_specs=[
            pl.BlockSpec(memory_space=pltpu.SMEM),
            pl.BlockSpec((sources, 1, places, width), lambda b: (0, b, 0, 0)),
        ],
        out_specs=[
            pl.BlockSpec((sources, 1, places, 2 * hd), lambda b: (0, b, 0, 0)),
            pl.BlockSpec((1, blocks, 2 * QB, 128), lambda b: (b, 0, 0, 0)),
        ],
        out_shape=[
            jax.ShapeDtypeStruct((sources, pairs, places, 2 * hd), BF16),
            jax.ShapeDtypeStruct((pairs, blocks, 2 * QB, 128), F32),
        ],
        scratch_shapes=[pltpu.VMEM((blocks, 2 * QB, QB), F32)],
        compiler_params=params(),
        name="attend",
    )(lengths, x)


def attend_back_kernel(
    len_ref, x_ref, do_ref, lse_ref, out_ref, dk_ref, dv_ref, p_ref, dp_ref
):
    sources, _, places, width = x_ref.shape
    hd = width // 4
    per = QB // places
    scale = hd**-0.5
    length = len_ref[pl.program_id(0)]
    blocks = sources * places // QB
    dk_ref[...] = jnp.zeros_like(dk_ref)
    dv_ref[...] = jnp.zeros_like(dv_ref)

    @pl.loop(0, blocks)
    def _(i):
        q = two_heads(x_ref, i, per, hd)
        do = two_heads(do_ref, i, per, hd)
        lse = lse_ref[0, i][:, 0:1]

        def weigh(kb, carry):
            total, delta = carry
            s = mm(q, one_head(x_ref, kb, per, hd, 2), NT) * scale
            p = jnp.where(allowed_at(i, kb, length, QB), jnp.exp(s - lse), 0.0)
            dp = mm(do, one_head(x_ref, kb, per, hd, 3), NT)
            p_ref[kb] = p
            dp_ref[kb] = dp
            pdp = p * dp
            for at in range(0, QB, 128):
                total = total + p[:, at : at + 128]
                delta = delta + pdp[:, at : at + 128]
            dv_ref[kb] += mm(p.astype(BF16), do, TN)
            return total, delta

        zero = jnp.zeros((2 * QB, 128), F32)
        total, delta = lax.fori_loop(0, i + 1, weigh, (zero, zero))
        delta = row_sum(delta) / row_sum(total)

        def spread(kb, dq):
            ds = (p_ref[kb] * (dp_ref[kb] - delta)).astype(BF16)
            dk_ref[kb] += mm(ds, q, TN)
            return dq + mm(ds, one_head(x_ref, kb, per, hd, 2))

        dq = lax.fori_loop(0, i + 1, spread, jnp.zeros((2 * QB, hd), F32))
        dq = (dq * scale).astype(BF16)
        out_ref[pl.ds(i * per, per), 0, :, 0:hd] = dq[:QB].reshape(per, places, hd)
        out_ref[pl.ds(i * per, per), 0, :, hd : 2 * hd] = dq[QB:].reshape(per, places, hd)

    @pl.loop(0, blocks)
    def _(i):
        dk = (dk_ref[i] * scale).astype(BF16)
        out_ref[pl.ds(i * per, per), 0, :, 2 * hd : 3 * hd] = dk.reshape(per, places, hd)
        out_ref[pl.ds(i * per, per), 0, :, 3 * hd :] = (
            dv_ref[i].astype(BF16).reshape(per, places, hd)
        )


def attend_back(lengths, x, do, lse):
    sources, pairs, places, width = x.shape
    hd = width // 4
    blocks = sources * places // QB
    return pl.pallas_call(
        attend_back_kernel,
        grid=(pairs,),
        in_specs=[
            pl.BlockSpec(memory_space=pltpu.SMEM),
            pl.BlockSpec((sources, 1, places, width), lambda b: (0, b, 0, 0)),
            pl.BlockSpec((sources, 1, places, 2 * hd), lambda b: (0, b, 0, 0)),
            pl.BlockSpec((1, blocks, 2 * QB, 128), lambda b: (b, 0, 0, 0)),
        ],
        out_specs=pl.BlockSpec((sources, 1, places, width), lambda b: (0, b, 0, 0)),
        out_shape=jax.ShapeDtypeStruct((sources, pairs, places, width), BF16),
        scratch_shapes=[
            pltpu.VMEM((blocks, QB, hd), F32),
            pltpu.VMEM((blocks, QB, hd), F32),
            pltpu.VMEM((blocks, 2 * QB, QB), F32),
            pltpu.VMEM((blocks, 2 * QB, QB), F32),
        ],
        compiler_params=params(),
        name="attend_back",
    )(lengths, x, do, lse)


def lane_in_back_one(lanes, coefs, static, dxn, gain, dcoef):
    x = joined(coefs, lanes)
    r = rsqrt_mean(x)
    xr = x * r
    dgain = dxn * xr
    e = dxn * gain
    dx = r * (e - xr * (row_sum(e * xr) * (1.0 / x.shape[1])))
    for i in range(LANES):
        dcoef = dcoef + row_sum(lanes[i] * dx) * lane_mask(8 * i)
    t = coefs - static
    return dx, dgain, dcoef, dcoef * (1.0 - t * t)


def lane_in_back_two(lane, alpha, dx, dhn, r, mean):
    return alpha * dx + r * (dhn - lane * (r * mean))


def group_mean(values, lane, width):
    return row_sum(values * group_mask(lane)) * (1.0 / width)


def middle_kernel(
    info_ref,
    h_ref,
    cot_ref,
    o_ref,
    ca_ref,
    wrow_ref,
    static_ref,
    gain_ref,
    weights_ref,
    out_ref,
    dh_ref,
    dca_ref,
    do_ref,
    xb_ref,
    dgu_ref,
    hid_ref,
    dyb_ref,
    dya_ref,
    dgain_ref,
    dhyper_ref,
    dstatic_ref,
    wo,
    wgu,
    wd,
    h1,
    ya,
    yb,
    gate,
    up,
    cb,
    zb,
    rb,
    raw,
    dcoef,
    sem,
):
    rows, width = xb_ref.shape
    groups = o_ref.shape[0]
    ff = hid_ref.shape[1]
    shards = wo.shape[0]
    out_rows, gu_rows, down_rows = wo.shape[1], wgu.shape[2], wd.shape[1]
    tiles = wgu.shape[0]
    half_tiles = tiles // 2
    chunks = rows // CHUNK

    def load(start, count, where, index):
        half = shards // 2
        return [
            pltpu.make_async_copy(
                weights_ref.at[:, z, pl.ds(start, count), :],
                where.at[pl.ds(z * half, half)],
                sem.at[2 * index + z],
            )
            for z in range(2)
        ]

    copies = [load(0, out_rows, wo, 0)]
    for t in range(tiles):
        copies.append(load(out_rows + t * gu_rows, gu_rows, wgu.at[t], 1 + t))
    copies.append(load(out_rows + tiles * gu_rows, down_rows, wd, 1 + tiles))
    for pair in copies:
        for copy in pair:
            copy.start()

    def arrive(pairs):
        for pair in pairs:
            for copy in pair:
                copy.wait()

    def chunk(step):
        return pl.ds(pl.multiple_of(step * CHUNK, CHUNK), CHUNK)

    tile = 256

    def tile_at(n):
        return pl.ds(pl.multiple_of(n * tile, tile), tile)

    arrive(copies[:1])

    @pl.loop(0, width // tile)
    def _(n):
        acc = 0.0
        for j in range(groups):
            span = o_ref.shape[2]
            per = span // out_rows
            w = wo[j * per : (j + 1) * per, :, tile_at(n)].reshape(span, tile)
            acc = acc + mm(o_ref[j], w)
        ya[:, tile_at(n)] = acc

    @pl.loop(0, chunks)
    def _(step):
        rs = chunk(step)
        lanes = lanes_of(h_ref, rs, width)
        coefs = ca_ref[rs, :]
        branch = ya[rs, :]
        new = []
        for j in range(LANES):
            new.append(mixed(coefs, lanes, j) + col(coefs, 8 * j + 5) * branch)
            h1[rs, j * width : (j + 1) * width] = new[j]
        rb[rs, :] = scale_pack(new)

    acc = 0.0
    for i in range(LANES):
        cs = slice(i * width, (i + 1) * width)
        for piece in two_parts(h1[:, cs]):
            acc = acc + mm(piece, wrow_ref[i], NT)
    raw[...] = acc

    @pl.loop(0, chunks)
    def _(step):
        rs = chunk(step)
        z = fold_low(raw[rs, :]) * rb[rs, :]
        coefs = jnp.tanh(z) + static_ref[...]
        cb[rs, :] = coefs
        zb[rs, :] = z
        x = joined(coefs, lanes_of(h1, rs, width))
        xb_ref[rs, :] = (x * rsqrt_mean(x) * gain_ref[...]).astype(BF16)

    arrive(copies[1:-1])
    for t in range(half_tiles):

        @pl.loop(0, width // tile)
        def _(n):
            x = xb_ref[...]
            cs = pl.ds(pl.multiple_of(t * width + n * tile, tile), tile)
            g = mm(x, wgu[t, :, :, tile_at(n)].reshape(width, tile))
            u = mm(x, wgu[half_tiles + t, :, :, tile_at(n)].reshape(width, tile))
            gate[:, cs] = g
            up[:, cs] = u
            hid_ref[:, cs] = (g / (1.0 + jnp.exp(-g)) * u).astype(BF16)

    arrive(copies[-1:])

    @pl.loop(0, width // tile)
    def _(n):
        yb[:, tile_at(n)] = mm(hid_ref[...], wd[:, :, tile_at(n)].reshape(ff, tile))

    @pl.loop(0, chunks)
    def _(step):
        rs = chunk(step)
        per_pair = rows // 2
        pair = step * CHUNK // per_pair
        place = info_ref[2] + lax.rem(step * CHUNK, per_pair)
        spot = place + lax.broadcasted_iota(jnp.int32, (CHUNK, 1), 0)
        valid = (spot < info_ref[pair]).astype(F32)
        lanes = lanes_of(h1, rs, width)
        coefs = cb[rs, :]
        branch = yb[rs, :]
        for j in range(LANES):
            new = mixed(coefs, lanes, j) + col(coefs, 8 * j + 5) * branch
            out_ref[rs, j * width : (j + 1) * width] = new.astype(BF16)
        grads = [g * valid for g in lanes_of(cot_ref, rs, width)]
        dcoef[rs, :] = mix_grads(lanes, grads, branch)
        dyb_ref[rs, :] = branch_grad(coefs, grads).astype(BF16)

    step_ff = 2 * down_rows

    @pl.loop(0, ff // step_ff)
    def _(s):
        cs = pl.ds(pl.multiple_of(s * step_ff, 128), step_ff)
        dhid = mm(dyb_ref[...], wd[pl.ds(2 * s, 2)].reshape(step_ff, width), NT)
        g = gate[:, cs]
        z = 1.0 / (1.0 + jnp.exp(-g))
        gz = g * z
        dgu_ref[:, cs] = (dhid * up[:, cs] * (z + gz * (1.0 - z))).astype(BF16)
        cs_up = pl.ds(pl.multiple_of(ff + s * step_ff, 128), step_ff)
        dgu_ref[:, cs_up] = (dhid * gz).astype(BF16)

    per = tile // gu_rows

    @pl.loop(0, width // tile)
    def _(n):
        acc = 0.0
        for t in range(tiles):
            w = wgu[t, pl.ds(n * per, per)].reshape(tile, width)
            acc = acc + mm(dgu_ref[:, t * width : (t + 1) * width], w, NT)
        yb[:, tile_at(n)] = acc

    dgain_ref[...] = jnp.zeros_like(dgain_ref)
    dstatic_ref[...] = jnp.zeros_like(dstatic_ref)

    @pl.loop(0, chunks)
    def _(step):
        rs = chunk(step)
        lanes = lanes_of(h1, rs, width)
        dx, dgain, dc, dt = lane_in_back_one(
            lanes, cb[rs, :], static_ref[...], yb[rs, :], gain_ref[...], dcoef[rs, :]
        )
        yb[rs, :] = dx
        dgain_ref[...] += fold8(dgain)
        dstatic_ref[...] += fold8(dc)
        dcoef[rs, :] = dt

    dt_low = split_pack(dcoef[...])
    dtr_low = split_pack(dcoef[...] * rb[...])
    dh_scr = gate
    for i in range(LANES):
        cs = slice(i * width, (i + 1) * width)
        part = hyper_rows(dtr_low, h1[:, cs].astype(BF16), i)
        if i == 0:
            dhyper_ref[...] = part
        else:
            dhyper_ref[...] += part
        dhn = mm(dt_low, wrow_ref[i])
        if i < LANES - 1:
            dh_scr[:, cs] = dhn
        else:
            up[:, 0:width] = dhn

    @pl.loop(0, chunks)
    def _(step):
        rs = chunk(step)
        per_pair = rows // 2
        pair = step * CHUNK // per_pair
        place = info_ref[2] + lax.rem(step * CHUNK, per_pair)
        spot = place + lax.broadcasted_iota(jnp.int32, (CHUNK, 1), 0)
        valid = (spot < info_ref[pair]).astype(F32)
        lanes = lanes_of(h1, rs, width)
        cots = [g * valid for g in lanes_of(cot_ref, rs, width)]
        coefs = cb[rs, :]
        dx = yb[rs, :]
        dtz = dcoef[rs, :] * zb[rs, :]
        scales = rb[rs, :]
        grads = []
        for i in range(LANES):
            if i < LANES - 1:
                dhn = dh_scr[rs, i * width : (i + 1) * width]
            else:
                dhn = up[rs, 0:width]
            back = lane_in_back_two(
                lanes[i], col(coefs, 8 * i), dx, dhn, col(scales, 8 * i), group_mean(dtz, i, width)
            )
            grads.append(unmixed(coefs, cots, i) + back)
        zero = lanes_of(h_ref, rs, width)
        coefs_a = ca_ref[rs, :]
        dca_ref[rs, :] = mix_grads(zero, grads, ya[rs, :])
        dya_ref[rs, :] = branch_grad(coefs_a, grads).astype(BF16)
        for i in range(LANES):
            dh_ref[rs, i * width : (i + 1) * width] = unmixed(coefs_a, grads, i)

    @pl.loop(0, groups)
    def _(j):
        span = o_ref.shape[2]
        per = span // out_rows
        w = wo[pl.ds(j * per, per)].reshape(span, width)
        do_ref[j] = mm(dya_ref[...], w, NT).astype(BF16)


def middle(info, h, cot, o, ca, wrow, static, gain, weights, out_rows, gu_rows, down_rows):
    rows, width4 = h.shape
    width = width4 // LANES
    shards = weights.shape[0] * weights.shape[1]
    ff = shards * down_rows
    tiles = 2 * ff // width
    groups, _, span = o.shape
    vm = pl.BlockSpec(memory_space=pltpu.VMEM)
    sds = jax.ShapeDtypeStruct
    return pl.pallas_call(
        middle_kernel,
        in_specs=[pl.BlockSpec(memory_space=pltpu.SMEM)]
        + [vm] * 7
        + [pl.BlockSpec(memory_space=pl.ANY)],
        out_specs=[vm] * 12,
        out_shape=[
            sds((rows, width4), BF16),
            sds((rows, width4), F32),
            sds((rows, PACK), F32),
            sds((groups, rows, span), BF16),
            sds((rows, width), BF16),
            sds((rows, 2 * ff), BF16),
            sds((rows, ff), BF16),
            sds((rows, width), BF16),
            sds((rows, width), BF16),
            sds((8, width), F32),
            sds((8, width), F32),
            sds((8, PACK), F32),
        ],
        scratch_shapes=[
            pltpu.VMEM((shards, out_rows, width), BF16),
            pltpu.VMEM((tiles, shards, gu_rows, width), BF16),
            pltpu.VMEM((shards, down_rows, width), BF16),
            pltpu.VMEM((rows, width4), F32),
            pltpu.VMEM((rows, width), F32),
            pltpu.VMEM((rows, width), F32),
            pltpu.VMEM((rows, ff), F32),
            pltpu.VMEM((rows, ff), F32),
            pltpu.VMEM((rows, PACK), F32),
            pltpu.VMEM((rows, PACK), F32),
            pltpu.VMEM((rows, PACK), F32),
            pltpu.VMEM((rows, PACK), F32),
            pltpu.VMEM((rows, PACK), F32),
            pltpu.SemaphoreType.DMA((2 * tiles + 4,)),
        ],
        compiler_params=params(),
        name="token_local",
    )(info, h, cot, o, ca, wrow, static, gain, weights)


def turn_back_kernel(
    d_ref, u_ref, x_ref, qg_ref, kg_ref, cos_ref, sin_ref, dqkv_ref, grad_ref, dqg_ref, dkg_ref
):
    hd = qg_ref.shape[1]
    rows = x_ref.shape[0]
    half_rows = rows // 2

    @pl.when(pl.program_id(0) == 0)
    def _():
        dqg_ref[...] = jnp.zeros_like(dqg_ref)
        dkg_ref[...] = jnp.zeros_like(dkg_ref)

    for part in range(2):
        rs = slice(part * half_rows, (part + 1) * half_rows)
        cos, sin = cos_ref[...], sin_ref[...]
        for k in range(3):
            cs = slice(k * hd, (k + 1) * hd)
            u = u_ref[0, rs, cs]
            dr = d_ref[0, rs, cs].astype(F32)
            dm = dr * cos - pltpu.roll(dr, hd // 2, 1) * sin
            r = rsqrt_mean(u)
            ur = u * r
            gain = qg_ref[...] if k < 2 else kg_ref[...]
            total = dqg_ref if k < 2 else dkg_ref
            total[...] += fold8(dm * ur)
            e = dm * gain
            du = r * (e - ur * (row_sum(e * ur) * (1.0 / hd)))
            dqkv_ref[0, rs, cs] = du.astype(BF16)
        dqkv_ref[0, rs, 3 * hd :] = d_ref[0, rs, 3 * hd :]
    half = x_ref.shape[1] // 2
    for z in range(2):
        grad = mm(x_ref[:, z * half : (z + 1) * half], dqkv_ref[0], TN)
        grad_ref[:, z] = grad.astype(BF16).reshape(grad_ref.shape[0], grad_ref.shape[2], 4 * hd)


def turn_back(d, u, x, q_gain, k_gain, cos, sin, shards):
    groups, rows, width4h = d.shape
    hd = width4h // 4
    width = x.shape[1]
    sds = jax.ShapeDtypeStruct

    def whole(a):
        return pl.BlockSpec(a.shape, lambda g: (0,) * a.ndim)

    return pl.pallas_call(
        turn_back_kernel,
        grid=(groups,),
        in_specs=[
            pl.BlockSpec((1, rows, 4 * hd), lambda g: (g, 0, 0)),
            pl.BlockSpec((1, rows, 3 * hd), lambda g: (g, 0, 0)),
        ]
        + [whole(a) for a in (x, q_gain, k_gain, cos, sin)],
        out_specs=[
            pl.BlockSpec((1, rows, 4 * hd), lambda g: (g, 0, 0)),
            pl.BlockSpec((shards // 2, 2, width // shards, 4 * hd), lambda g: (0, 0, 0, g)),
            pl.BlockSpec((8, hd), lambda g: (0, 0)),
            pl.BlockSpec((8, hd), lambda g: (0, 0)),
        ],
        out_shape=[
            sds((groups, rows, 4 * hd), BF16),
            sds((shards // 2, 2, width // shards, groups * 4 * hd), BF16),
            sds((8, hd), F32),
            sds((8, hd), F32),
        ],
        compiler_params=params(),
        name="rotary_back",
    )(d, u, x, q_gain, k_gain, cos, sin)


def last_kernel(
    dqkv_ref,
    w_ref,
    h_ref,
    c_ref,
    z_ref,
    dc_ref,
    dh_ref,
    wrow_ref,
    static_ref,
    gain_ref,
    dres_ref,
    dgain_ref,
    dhyper_ref,
    dstatic_ref,
    dx_ref,
    dt_ref,
    r_ref,
):
    groups, rows, span = dqkv_ref.shape
    width = gain_ref.shape[1]
    tile = 256

    per = tile // w_ref.shape[2]
    half_tiles = width // tile // 2

    @pl.loop(0, width // tile)
    def _(n):
        z, at = n // half_tiles, lax.rem(n, half_tiles) * per
        acc = 0.0
        for g in range(groups):
            w = w_ref[pl.ds(at, per), z, :, g * span : (g + 1) * span].reshape(tile, span)
            acc = acc + mm(dqkv_ref[g], w, NT)
        dx_ref[:, pl.ds(pl.multiple_of(n * tile, tile), tile)] = acc

    dgain_ref[...] = jnp.zeros_like(dgain_ref)
    dstatic_ref[...] = jnp.zeros_like(dstatic_ref)

    def chunk(step):
        return pl.ds(pl.multiple_of(step * CHUNK, CHUNK), CHUNK)

    @pl.loop(0, rows // CHUNK)
    def _(step):
        rs = chunk(step)
        lanes = lanes_of(h_ref, rs, width)
        dx, dgain, dc, dt = lane_in_back_one(
            lanes, c_ref[rs, :], static_ref[...], dx_ref[rs, :], gain_ref[...], dc_ref[rs, :]
        )
        dx_ref[rs, :] = dx
        dgain_ref[...] += fold8(dgain)
        dstatic_ref[...] += fold8(dc)
        dt_ref[rs, :] = dt
        r_ref[rs, :] = scale_pack(lanes)

    dt_low = split_pack(dt_ref[...])
    dtr_low = split_pack(dt_ref[...] * r_ref[...])
    for i in range(LANES):
        cs = slice(i * width, (i + 1) * width)
        part = hyper_rows(dtr_low, h_ref[:, cs], i)
        if i == 0:
            dhyper_ref[...] = part
        else:
            dhyper_ref[...] += part
        dres_ref[:, cs] = mm(dt_low, wrow_ref[i])

    @pl.loop(0, rows // CHUNK)
    def _(step):
        rs = chunk(step)
        coefs = c_ref[rs, :]
        dx = dx_ref[rs, :]
        dtz = dt_ref[rs, :] * z_ref[rs, :]
        scales = r_ref[rs, :]
        for i in range(LANES):
            cs = slice(i * width, (i + 1) * width)
            lane = h_ref[rs, cs].astype(F32)
            back = lane_in_back_two(
                lane,
                col(coefs, 8 * i),
                dx,
                dres_ref[rs, cs],
                col(scales, 8 * i),
                group_mean(dtz, i, width),
            )
            dres_ref[rs, cs] = dh_ref[rs, cs] + back


def last(dqkv, w_grouped, h, c, z, dc, dh, wrow, static, gain):
    rows, width4 = h.shape
    width = width4 // LANES
    vm = pl.BlockSpec(memory_space=pltpu.VMEM)
    sds = jax.ShapeDtypeStruct
    return pl.pallas_call(
        last_kernel,
        in_specs=[vm] * 10,
        out_specs=[vm] * 4,
        out_shape=[
            sds((rows, width4), F32),
            sds((8, width), F32),
            sds((8, width), F32),
            sds((8, PACK), F32),
        ],
        scratch_shapes=[
            pltpu.VMEM((rows, width), F32),
            pltpu.VMEM((rows, PACK), F32),
            pltpu.VMEM((rows, PACK), F32),
        ],
        compiler_params=params(),
        name="lane_in_back",
    )(dqkv, w_grouped, h, c, z, dc, dh, wrow, static, gain)


def grads_kernel(o_ref, dya_ref, xb_ref, dgu_ref, hid_ref, dyb_ref, out_ref):
    per, _, owned, width = out_ref.shape
    out_rows = o_ref.shape[0] * o_ref.shape[2] // per
    gu_rows = xb_ref.shape[1] // per
    down_rows = hid_ref.shape[1] // per
    tiles = dgu_ref.shape[1] // width
    piece = mm(hid_ref[...], dyb_ref[...], TN).astype(BF16)
    for s in range(per):
        at = out_rows + tiles * gu_rows
        out_ref[s, 0, at : at + down_rows, :] = piece[s * down_rows : (s + 1) * down_rows]
    for j in range(o_ref.shape[0]):
        piece = mm(o_ref[j], dya_ref[...], TN).astype(BF16)
        heads = o_ref.shape[2] // out_rows
        for s in range(heads):
            out_ref[j * heads + s, 0, 0:out_rows, :] = piece[s * out_rows : (s + 1) * out_rows]

    for t in range(tiles):
        cs = slice(t * width, (t + 1) * width)
        piece = mm(xb_ref[...], dgu_ref[:, cs], TN).astype(BF16)
        for s in range(per):
            at = out_rows + t * gu_rows
            out_ref[s, 0, at : at + gu_rows, :] = piece[s * gu_rows : (s + 1) * gu_rows]


def weight_grads(o, dya, xb, dgu, hid, dyb, shards):
    rows, width = xb.shape
    ff = hid.shape[1]
    groups, _, span = o.shape
    steps = 4
    per = shards // steps
    owned = (groups * span + 3 * ff) // shards
    return pl.pallas_call(
        grads_kernel,
        grid=(steps,),
        in_specs=[
            pl.BlockSpec((groups // steps, rows, span), lambda g: (g, 0, 0)),
            pl.BlockSpec((rows, width), lambda g: (0, 0)),
            pl.BlockSpec((rows, width // steps), lambda g: (0, g)),
            pl.BlockSpec((rows, 2 * ff), lambda g: (0, 0)),
            pl.BlockSpec((rows, ff // steps), lambda g: (0, g)),
            pl.BlockSpec((rows, width), lambda g: (0, 0)),
        ],
        out_specs=pl.BlockSpec((per, 1, owned, width), lambda g: (g % 2, g // 2, 0, 0)),
        out_shape=jax.ShapeDtypeStruct((shards // 2, 2, owned, width), BF16),
        compiler_params=params(),
        name="weight_grads",
    )(o, dya, xb, dgu, hid, dyb)


RING = 4


def pair_along(kind, count, stride):
    pairs = []
    for i in range(count):
        at = i // stride % RING
        to = at ^ 1 if kind == 0 else RING - 1 - at
        pairs.append((i, i + (to - at) * stride))
    return pairs


def swap_y(values, kind):
    return lax.ppermute(values, "rep", pair_along(kind, lax.axis_size("rep"), 1))


def swap_z(values, kind):
    rep, shard = lax.axis_size("rep"), lax.axis_size("shard")
    pairs = []
    for r in range(rep):
        for s in range(shard):
            z = 2 * (r // RING) + s // (shard // 2)
            to = z ^ 1 if kind == 0 else 3 - z
            target = (to // 2 * RING + r % RING) * shard + to % 2 * (shard // 2) + s % (shard // 2)
            pairs.append((r * shard + s, target))
    return lax.ppermute(values, ("rep", "shard"), pairs)


def z_place():
    return lax.axis_index("shard") // (lax.axis_size("shard") // 2)


def z_groups():
    half = lax.axis_size("shard") // 2
    return [list(range(half)), list(range(half, 2 * half))]


def gather_rows(block):
    mid = block.shape[1] // 2
    other = jnp.concatenate([swap_z(block[:, :mid], 0), swap_z(block[:, mid:], 1)], axis=1)
    first = z_place() == 0
    pair = jnp.stack([jnp.where(first, block, other), jnp.where(first, other, block)])
    return lax.all_gather(pair, "shard", axis_index_groups=z_groups())


def scatter_rows(parts):
    return lax.psum_scatter(
        parts, "shard", scatter_dimension=0, axis_index_groups=z_groups(), tiled=False
    )


def swap_xor(values, axis, stride):
    return lax.ppermute(values, axis, [(i, i ^ stride) for i in range(lax.axis_size(axis))])


def rep_sum(pair):
    first = z_place() == 0
    values = jnp.where(first, pair[0], pair[1])
    others = jnp.where(first, pair[1], pair[0])
    place = lax.axis_index("rep") % RING
    bits = [(place % 2 + place // 2) % 2, place // 2]
    mid = values.shape[1] // 2
    orders = ((0, 1), (1, 0))
    spans = (slice(0, mid), slice(mid, None))
    got = yield [(partial(swap_z, kind=o[0]), others[:, cs]) for o, cs in zip(orders, spans)]
    acc = [values[:, cs].astype(F32) + g.astype(F32) for cs, g in zip(spans, got)]
    half = values.shape[0]
    for step in range(2):
        half //= 2
        keep, give = [], []
        for o, a in zip(orders, acc):
            bit = bits[o[step]]
            keep.append(lax.dynamic_slice_in_dim(a, bit * half, half, 0))
            give.append(lax.dynamic_slice_in_dim(a, (1 - bit) * half, half, 0).astype(BF16))
        got = yield [(partial(swap_y, kind=o[step]), g) for o, g in zip(orders, give)]
        acc = [k + g.astype(F32) for k, g in zip(keep, got)]
    low = [a.astype(BF16) for a in acc]
    got = yield [(partial(swap_xor, axis="rep", stride=RING), v) for v in low]
    low = [(v.astype(F32) + g.astype(F32)).astype(BF16) for v, g in zip(low, got)]
    for step in (1, 0):
        got = yield [(partial(swap_y, kind=o[step]), v) for o, v in zip(orders, low)]
        for n, (o, g) in enumerate(zip(orders, got)):
            mine = bits[o[step]] == 0
            low[n] = jnp.concatenate(
                [jnp.where(mine, low[n], g), jnp.where(mine, g, low[n])], axis=0
            )
    return jnp.concatenate(low, axis=1)


def sum_everywhere(values):
    pairs = partial(pair_along, count=lax.axis_size("shard"), stride=2)
    swaps = [partial(swap_y, kind=0), partial(swap_y, kind=1)]
    swaps += [partial(swap_xor, axis="rep", stride=RING), partial(swap_xor, axis="shard", stride=1)]
    swaps += [lambda v, k=k: lax.ppermute(v, "shard", pairs(k)) for k in (0, 1)]
    swaps += [partial(swap_xor, axis="shard", stride=2 * RING)]
    for swap in swaps:
        (got,) = yield [(swap, values)]
        values = values + got
    return values


def rounds(*chains):
    results = [None] * len(chains)
    asked = {n: next(chain) for n, chain in enumerate(chains)}
    while asked:
        got = {n: [swap(value) for swap, value in wants] for n, wants in asked.items()}
        got = lax.optimization_barrier(got)
        asked = {}
        for n, values in got.items():
            try:
                asked[n] = chains[n].send(values)
            except StopIteration as end:
                results[n] = end.value
    return results


def rotary_tables(first, count, head_dim):
    half_dim = head_dim // 2
    inverse = ROTARY_BASE ** (-jnp.arange(half_dim, dtype=F32) * 2.0 / head_dim)
    places = (first + jnp.arange(count, dtype=jnp.int32)).astype(F32)
    angles = places[:, None] * inverse[None, :]
    cos, sin = jnp.cos(angles), jnp.sin(angles)
    return jnp.concatenate([cos, cos], axis=1), jnp.concatenate([-sin, sin], axis=1)


def packed_static(static):
    lanes, count = static.shape
    flat = jnp.pad(static, ((0, 0), (0, 8 - count))).reshape(1, lanes * 8)
    return jnp.pad(flat, ((0, 0), (0, PACK - lanes * 8)))


def on_device(
    residuals,
    lengths,
    w_query,
    w_key,
    w_value,
    w_out,
    w_gate,
    w_up,
    w_down,
    attn_gain,
    mlp_gain,
    query_gain,
    key_gain,
    hyper_weight,
    hyper_static,
    cotangent,
):
    pairs, places, lane_count, width = residuals.shape
    rows = pairs * places
    hd = query_gain.shape[0]
    rep = lax.axis_size("rep")
    shards = lax.axis_size("shard")
    local = w_query.shape[0]
    groups = w_key.shape[1] // hd
    ff = w_gate.shape[1]
    tiles = ff // width
    first = lax.axis_index("rep") * places

    grouped = jnp.concatenate(
        [
            w_query.reshape(local, groups, 2 * hd),
            w_key.reshape(local, groups, hd),
            w_value.reshape(local, groups, hd),
        ],
        axis=2,
    ).reshape(local, groups * 4 * hd)
    w_grouped = gather_rows(grouped)
    rest = jnp.concatenate(
        [w_out]
        + [w_gate[:, t * width : (t + 1) * width] for t in range(tiles)]
        + [w_up[:, t * width : (t + 1) * width] for t in range(tiles)]
        + [w_down],
        axis=0,
    )
    w_rest = gather_rows(rest)

    h = residuals.reshape(rows, lane_count * width)
    cot = cotangent.reshape(rows, lane_count * width)
    wrow = pack(hyper_weight)
    wrow_a, wrow_b = wrow[0], wrow[1]
    static_a, static_b = packed_static(hyper_static[0]), packed_static(hyper_static[1])
    gain_a, gain_b = attn_gain[None, :], mlp_gain[None, :]
    q_gain, k_gain = query_gain[None, :], key_gain[None, :]
    cos, sin = rotary_tables(first, places, hd)
    info = jnp.concatenate([lengths, first[None].astype(jnp.int32)])

    xa, ca, za = pre(h, wrow_a, static_a, gain_a)
    send, keep = qkv(xa, w_grouped, q_gain, k_gain, cos, sin)
    x = lax.all_to_all(send, "rep", 0, 0, tiled=True).reshape(rep, pairs, places, 4 * hd)
    o_own, lse = attend(lengths, x)
    o = lax.all_to_all(o_own.reshape(rep, rows, 2 * hd), "rep", 0, 0, tiled=True)
    (out, dh, dca, do, xb, dgu, hid, dyb, dya, dgain_b, dhyper_b, dstatic_b) = middle(
        info,
        h,
        cot,
        o,
        ca,
        wrow_b,
        static_b,
        gain_b,
        w_rest,
        w_out.shape[0],
        local,
        w_down.shape[0],
    )
    rest_part = weight_grads(o, dya, xb, dgu, hid, dyb, shards)
    do, rest_part = lax.optimization_barrier((do, rest_part))
    do_own = lax.all_to_all(do, "rep", 0, 0, tiled=True).reshape(rep, pairs, places, 2 * hd)
    rest_own = scatter_rows(rest_part)
    d_own = attend_back(lengths, x, do_own, lse)
    d = lax.all_to_all(d_own.reshape(rep, rows, 4 * hd), "rep", 0, 0, tiled=True)
    dqkv, qkv_part, dqg, dkg = turn_back(d, keep, xa, q_gain, k_gain, cos, sin, shards)
    dres, dgain_a, dhyper_a, dstatic_a = last(
        dqkv, w_grouped, h, ca, za, dca, dh, wrow_a, static_a, gain_a
    )
    count = hyper_weight.shape[1]
    small = jnp.concatenate(
        [
            dgain_a.sum(0),
            dgain_b.sum(0),
            dqg.sum(0),
            dkg.sum(0),
            dhyper_a[:count].reshape(-1),
            dhyper_b[:count].reshape(-1),
            dstatic_a.sum(0),
            dstatic_b.sum(0),
        ]
    ).reshape(-1, PACK)
    qkv_part, rest_own, dres, small = lax.optimization_barrier((qkv_part, rest_own, dres, small))
    qkv_own = scatter_rows(qkv_part)
    rest_low, small = rounds(rep_sum(rest_own), sum_everywhere(small))
    rest_sum = rest_low.astype(F32)
    at, edge = w_out.shape[0], w_out.shape[0] + 2 * tiles * local
    gu = rest_sum[at:edge].reshape(2, tiles, local, width).transpose(0, 2, 1, 3)
    gu = gu.reshape(2, local, ff)
    small = small.reshape(-1)
    (qkv_low,) = rounds(rep_sum(qkv_own))
    qkv_sum = qkv_low.astype(F32).reshape(local, groups, 4 * hd)
    sizes = [width, width, hd, hd, count * width, count * width, PACK, PACK]
    pieces, start = [], 0
    for size in sizes:
        pieces.append(small[start : start + size])
        start += size

    def unpack(flat):
        return flat[: 8 * lane_count].reshape(lane_count, 8)[:, :count]

    return (
        out.reshape(residuals.shape),
        dres.reshape(residuals.shape),
        qkv_sum[:, :, : 2 * hd].reshape(local, -1),
        qkv_sum[:, :, 2 * hd : 3 * hd].reshape(local, -1),
        qkv_sum[:, :, 3 * hd :].reshape(local, -1),
        rest_sum[:at],
        gu[0],
        gu[1],
        rest_sum[edge:],
        pieces[0],
        pieces[1],
        pieces[2],
        pieces[3],
        jnp.stack([pieces[4].reshape(count, width), pieces[5].reshape(count, width)]),
        jnp.stack([unpack(pieces[6]), unpack(pieces[7])]),
    )


def solution(mesh):
    lane_spec = P("shard", "rep", None, None)
    row_spec = P("shard", None)
    in_specs = (lane_spec, P("shard")) + (row_spec,) * 7 + (P(),) * 6 + (lane_spec,)
    out_specs = (lane_spec, lane_spec) + (row_spec,) * 7 + (P(),) * 6
    return jax.shard_map(
        on_device, mesh=mesh, in_specs=in_specs, out_specs=out_specs, check_vma=False
    )
```

```python
from functools import partial

import jax
import jax.numpy as jnp
from jax import lax
from jax.experimental import pallas as pl
from jax.experimental.pallas import tpu as pltpu
from jax.sharding import PartitionSpec as P

EPSILON = 1e-06
ROTARY_BASE = 1000000.0
MASKED = -1e30
LANES = 4
SPAN = 32
PACK = 128
NT = (((1,), (1,)), ((), ()))
NN = (((1,), (0,)), ((), ()))
TN = (((0,), (0,)), ((), ()))
F32 = jnp.float32
BF16 = jnp.bfloat16
VMEM_LIMIT = 60 * 1024 * 1024
CHUNK = 64


def mm(a, b, dims=NN):
    return lax.dot_general(a, b, dims, preferred_element_type=F32)


def params(limit=VMEM_LIMIT):
    return pltpu.CompilerParams(vmem_limit_bytes=limit)


def lane_mask(column):
    spot = lax.broadcasted_iota(jnp.int32, (1, PACK), 1)
    return (spot == column).astype(F32)


def group_mask(lane):
    spot = lax.broadcasted_iota(jnp.int32, (1, PACK), 1)
    return (spot // 8 == lane).astype(F32)


def row_sum(values):
    return jnp.sum(values, axis=1, keepdims=True)


def col(coefs, index):
    return coefs[:, index : index + 1]


def rsqrt_mean(values):
    return lax.rsqrt(row_sum(values * values) * (1.0 / values.shape[1]) + EPSILON)


def lanes_of(ref, rows, width):
    return [ref[rows, i * width : (i + 1) * width].astype(F32) for i in range(LANES)]


def scale_pack(lanes):
    out = 0.0
    for i, h in enumerate(lanes):
        out = out + rsqrt_mean(h) * group_mask(i)
    return out


def mixed(coefs, lanes, j):
    out = col(coefs, 1 + j) * lanes[0]
    for i in range(1, LANES):
        out = out + col(coefs, 8 * i + 1 + j) * lanes[i]
    return out


def unmixed(coefs, grads, i):
    out = col(coefs, 8 * i + 1) * grads[0]
    for j in range(1, LANES):
        out = out + col(coefs, 8 * i + 1 + j) * grads[j]
    return out


def joined(coefs, lanes):
    out = col(coefs, 0) * lanes[0]
    for i in range(1, LANES):
        out = out + col(coefs, 8 * i) * lanes[i]
    return out


def branch_grad(coefs, grads):
    out = col(coefs, 5) * grads[0]
    for j in range(1, LANES):
        out = out + col(coefs, 8 * j + 5) * grads[j]
    return out


def mix_grads(lanes, grads, branch):
    out = 0.0
    for j in range(LANES):
        for i in range(LANES):
            out = out + row_sum(lanes[i] * grads[j]) * lane_mask(8 * i + 1 + j)
        out = out + row_sum(branch * grads[j]) * lane_mask(8 * j + 5)
    return out


def fold_low(raw):
    return raw + (pltpu.roll(raw, PACK - 2 * SPAN, 1) + pltpu.roll(raw, PACK - 3 * SPAN, 1))


def two_parts(values):
    high = values.astype(BF16)
    return high, (values - high.astype(F32)).astype(BF16)


def split_pack(values):
    high = values.astype(BF16).astype(F32)
    return (high + pltpu.roll(values - high, SPAN, 1) + pltpu.roll(high, 2 * SPAN, 1)).astype(BF16)


def hyper_rows(dtr_pack, lane_low, i):
    full = mm(dtr_pack, lane_low, TN)
    return full[8 * i : 8 * i + 8] + full[SPAN + 8 * i : SPAN + 8 * i + 8]


def fold8(values):
    rows = values.shape[0]
    out = values[0:8]
    for at in range(8, rows, 8):
        out = out + values[at : at + 8]
    return out


def pack_kernel(w_ref, out_ref):
    layers, count, width = w_ref.shape
    blank = jnp.zeros((8, width), F32)
    for layer in range(layers):
        w = jnp.concatenate([w_ref[layer], jnp.zeros((8 - count, width), F32)], axis=0)
        high = w.astype(BF16).astype(F32)
        for i in range(LANES):
            pieces = [blank] * (PACK // 8)
            pieces[i] = pieces[SPAN // 8 + i] = high
            pieces[2 * SPAN // 8 + i] = low = (w - high).astype(BF16).astype(F32)
            pieces[3 * SPAN // 8 + i] = (w - high) - low
            out_ref[layer, i] = jnp.concatenate(pieces, axis=0).astype(BF16)


def pack(hyper_weight):
    layers, _, width = hyper_weight.shape
    vm = pl.BlockSpec(memory_space=pltpu.VMEM)
    return pl.pallas_call(
        pack_kernel,
        in_specs=[vm],
        out_specs=vm,
        out_shape=jax.ShapeDtypeStruct((layers, LANES, PACK, width), BF16),
        compiler_params=params(),
        name="pack_hyper_weights",
    )(hyper_weight)


def pre_kernel(h_ref, w_ref, static_ref, gain_ref, x_ref, coef_ref, z_ref, raw_ref):
    rows, width = x_ref.shape
    acc = 0.0
    for i in range(LANES):
        acc = acc + mm(h_ref[:, i * width : (i + 1) * width], w_ref[i], NT)
    raw_ref[...] = acc

    @pl.loop(0, rows // CHUNK)
    def _(step):
        rs = pl.ds(pl.multiple_of(step * CHUNK, CHUNK), CHUNK)
        lanes = lanes_of(h_ref, rs, width)
        z = fold_low(raw_ref[rs, :]) * scale_pack(lanes)
        coefs = jnp.tanh(z) + static_ref[...]
        x = joined(coefs, lanes)
        x_ref[rs, :] = (x * rsqrt_mean(x) * gain_ref[...]).astype(BF16)
        coef_ref[rs, :] = coefs
        z_ref[rs, :] = z


def pre(h, wrow, static, gain):
    rows, width4 = h.shape
    width = width4 // LANES
    block = rows // 2
    return pl.pallas_call(
        pre_kernel,
        grid=(2,),
        in_specs=[
            pl.BlockSpec((block, width4), lambda g: (g, 0)),
            pl.BlockSpec((LANES, PACK, width), lambda g: (0, 0, 0)),
            pl.BlockSpec((1, PACK), lambda g: (0, 0)),
            pl.BlockSpec((1, width), lambda g: (0, 0)),
        ],
        out_specs=[
            pl.BlockSpec((block, width), lambda g: (g, 0)),
            pl.BlockSpec((block, PACK), lambda g: (g, 0)),
            pl.BlockSpec((block, PACK), lambda g: (g, 0)),
        ],
        out_shape=[
            jax.ShapeDtypeStruct((rows, width), BF16),
            jax.ShapeDtypeStruct((rows, PACK), F32),
            jax.ShapeDtypeStruct((rows, PACK), F32),
        ],
        scratch_shapes=[pltpu.VMEM((block, PACK), F32)],
        compiler_params=params(),
        name="lane_in_zero",
    )(h, wrow, static, gain)


def rotate(u, gain, cos, sin_signed):
    half = u.shape[1] // 2
    m = u * rsqrt_mean(u) * gain
    return m * cos + pltpu.roll(m, half, 1) * sin_signed


def qkv_kernel(x_ref, w_ref, qg_ref, kg_ref, cos_ref, sin_ref, send_ref, keep_ref):
    hd = qg_ref.shape[1]
    rows = x_ref.shape[0]
    half = x_ref.shape[1] // 2
    u = 0.0
    for z in range(2):
        w = w_ref[:, z].reshape(half, 4 * hd)
        u = u + mm(x_ref[:, z * half : (z + 1) * half], w)
    half_rows = rows // 2
    for part in range(2):
        rs = slice(part * half_rows, (part + 1) * half_rows)
        cos, sin = cos_ref[...], sin_ref[...]
        for k in range(3):
            cs = slice(k * hd, (k + 1) * hd)
            piece = u[rs, cs]
            keep_ref[0, rs, cs] = piece
            gain = qg_ref[...] if k < 2 else kg_ref[...]
            send_ref[0, rs, cs] = rotate(piece, gain, cos, sin).astype(BF16)
        send_ref[0, rs, 3 * hd :] = u[rs, 3 * hd :].astype(BF16)


def qkv(x, w_grouped, q_gain, k_gain, cos, sin_signed):
    rows, width = x.shape
    hd = q_gain.shape[1]
    groups = w_grouped.shape[3] // (4 * hd)
    return pl.pallas_call(
        qkv_kernel,
        grid=(groups,),
        in_specs=[
            pl.BlockSpec((rows, width), lambda g: (0, 0)),
            pl.BlockSpec(w_grouped.shape[:3] + (4 * hd,), lambda g: (0, 0, 0, g)),
            pl.BlockSpec((1, hd), lambda g: (0, 0)),
            pl.BlockSpec((1, hd), lambda g: (0, 0)),
            pl.BlockSpec(cos.shape, lambda g: (0, 0)),
            pl.BlockSpec(cos.shape, lambda g: (0, 0)),
        ],
        out_specs=[
            pl.BlockSpec((1, rows, 4 * hd), lambda g: (g, 0, 0)),
            pl.BlockSpec((1, rows, 3 * hd), lambda g: (g, 0, 0)),
        ],
        out_shape=[
            jax.ShapeDtypeStruct((groups, rows, 4 * hd), BF16),
            jax.ShapeDtypeStruct((groups, rows, 3 * hd), F32),
        ],
        compiler_params=params(),
        name="qkv_rotary",
    )(x, w_grouped, q_gain, k_gain, cos, sin_signed)


QB = 256


def allowed_at(i, kb, length, block):
    row = lax.broadcasted_iota(jnp.int32, (2 * block, block), 0)
    row = jnp.where(row >= block, row - block, row) + i * block
    key = lax.broadcasted_iota(jnp.int32, (2 * block, block), 1) + kb * block
    return (key <= row) & (key < length)


def two_heads(ref, i, per, hd, at=0):
    first = ref[pl.ds(i * per, per), 0, :, at * hd : (at + 1) * hd]
    second = ref[pl.ds(i * per, per), 0, :, (at + 1) * hd : (at + 2) * hd]
    return jnp.concatenate([first.reshape(-1, hd), second.reshape(-1, hd)], axis=0)


def one_head(ref, i, per, hd, at):
    return ref[pl.ds(i * per, per), 0, :, at * hd : (at + 1) * hd].reshape(-1, hd)


def attend_kernel(len_ref, x_ref, o_ref, lse_ref, s_ref):
    sources, _, places, width = x_ref.shape
    hd = width // 4
    per = QB // places
    scale = hd**-0.5
    length = len_ref[pl.program_id(0)]

    @pl.loop(0, sources * places // QB)
    def _(i):
        q = two_heads(x_ref, i, per, hd)

        def score(kb, top):
            s = mm(q, one_head(x_ref, kb, per, hd, 2), NT) * scale
            s = jnp.where(allowed_at(i, kb, length, QB), s, MASKED)
            s_ref[kb] = s
            for at in range(0, QB, 128):
                top = jnp.maximum(top, s[:, at : at + 128])
            return top

        top = lax.fori_loop(0, i + 1, score, jnp.full((2 * QB, 128), MASKED, F32))
        top = jnp.max(top, axis=1, keepdims=True)

        def weigh(kb, total):
            p = jnp.exp(s_ref[kb] - top)
            s_ref[kb] = p
            for at in range(0, QB, 128):
                total = total + p[:, at : at + 128]
            return total

        total = row_sum(lax.fori_loop(0, i + 1, weigh, jnp.zeros((2 * QB, 128), F32)))
        inverse = 1.0 / total

        def gather(kb, acc):
            p = (s_ref[kb] * inverse).astype(BF16)
            return acc + mm(p, one_head(x_ref, kb, per, hd, 3))

        o = lax.fori_loop(0, i + 1, gather, jnp.zeros((2 * QB, hd), F32)).astype(BF16)
        lse_ref[0, i] = jnp.broadcast_to(top + jnp.log(total), (2 * QB, 128))
        o_ref[pl.ds(i * per, per), 0, :, 0:hd] = o[:QB].reshape(per, places, hd)
        o_ref[pl.ds(i * per, per), 0, :, hd:] = o[QB:].reshape(per, places, hd)


def attend(lengths, x):
    sources, pairs, places, width = x.shape
    hd = width // 4
    blocks = sources * places // QB
    return pl.pallas_call(
        attend_kernel,
        grid=(pairs,),
        in_specs=[
            pl.BlockSpec(memory_space=pltpu.SMEM),
            pl.BlockSpec((sources, 1, places, width), lambda b: (0, b, 0, 0)),
        ],
        out_specs=[
            pl.BlockSpec((sources, 1, places, 2 * hd), lambda b: (0, b, 0, 0)),
            pl.BlockSpec((1, blocks, 2 * QB, 128), lambda b: (b, 0, 0, 0)),
        ],
        out_shape=[
            jax.ShapeDtypeStruct((sources, pairs, places, 2 * hd), BF16),
            jax.ShapeDtypeStruct((pairs, blocks, 2 * QB, 128), F32),
        ],
        scratch_shapes=[pltpu.VMEM((blocks, 2 * QB, QB), F32)],
        compiler_params=params(),
        name="attend",
    )(lengths, x)


def attend_back_kernel(
    len_ref, x_ref, do_ref, lse_ref, out_ref, dk_ref, dv_ref, p_ref, dp_ref
):
    sources, _, places, width = x_ref.shape
    hd = width // 4
    per = QB // places
    scale = hd**-0.5
    length = len_ref[pl.program_id(0)]
    blocks = sources * places // QB
    dk_ref[...] = jnp.zeros_like(dk_ref)
    dv_ref[...] = jnp.zeros_like(dv_ref)

    @pl.loop(0, blocks)
    def _(i):
        q = two_heads(x_ref, i, per, hd)
        do = two_heads(do_ref, i, per, hd)
        lse = lse_ref[0, i][:, 0:1]

        def weigh(kb, carry):
            total, delta = carry
            s = mm(q, one_head(x_ref, kb, per, hd, 2), NT) * scale
            p = jnp.where(allowed_at(i, kb, length, QB), jnp.exp(s - lse), 0.0)
            dp = mm(do, one_head(x_ref, kb, per, hd, 3), NT)
            p_ref[kb] = p
            dp_ref[kb] = dp
            pdp = p * dp
            for at in range(0, QB, 128):
                total = total + p[:, at : at + 128]
                delta = delta + pdp[:, at : at + 128]
            dv_ref[kb] += mm(p.astype(BF16), do, TN)
            return total, delta

        zero = jnp.zeros((2 * QB, 128), F32)
        total, delta = lax.fori_loop(0, i + 1, weigh, (zero, zero))
        delta = row_sum(delta) / row_sum(total)

        def spread(kb, dq):
            ds = (p_ref[kb] * (dp_ref[kb] - delta)).astype(BF16)
            dk_ref[kb] += mm(ds, q, TN)
            return dq + mm(ds, one_head(x_ref, kb, per, hd, 2))

        dq = lax.fori_loop(0, i + 1, spread, jnp.zeros((2 * QB, hd), F32))
        dq = (dq * scale).astype(BF16)
        out_ref[pl.ds(i * per, per), 0, :, 0:hd] = dq[:QB].reshape(per, places, hd)
        out_ref[pl.ds(i * per, per), 0, :, hd : 2 * hd] = dq[QB:].reshape(per, places, hd)

    @pl.loop(0, blocks)
    def _(i):
        dk = (dk_ref[i] * scale).astype(BF16)
        out_ref[pl.ds(i * per, per), 0, :, 2 * hd : 3 * hd] = dk.reshape(per, places, hd)
        out_ref[pl.ds(i * per, per), 0, :, 3 * hd :] = (
            dv_ref[i].astype(BF16).reshape(per, places, hd)
        )


def attend_back(lengths, x, do, lse):
    sources, pairs, places, width = x.shape
    hd = width // 4
    blocks = sources * places // QB
    return pl.pallas_call(
        attend_back_kernel,
        grid=(pairs,),
        in_specs=[
            pl.BlockSpec(memory_space=pltpu.SMEM),
            pl.BlockSpec((sources, 1, places, width), lambda b: (0, b, 0, 0)),
            pl.BlockSpec((sources, 1, places, 2 * hd), lambda b: (0, b, 0, 0)),
            pl.BlockSpec((1, blocks, 2 * QB, 128), lambda b: (b, 0, 0, 0)),
        ],
        out_specs=pl.BlockSpec((sources, 1, places, width), lambda b: (0, b, 0, 0)),
        out_shape=jax.ShapeDtypeStruct((sources, pairs, places, width), BF16),
        scratch_shapes=[
            pltpu.VMEM((blocks, QB, hd), F32),
            pltpu.VMEM((blocks, QB, hd), F32),
            pltpu.VMEM((blocks, 2 * QB, QB), F32),
            pltpu.VMEM((blocks, 2 * QB, QB), F32),
        ],
        compiler_params=params(),
        name="attend_back",
    )(lengths, x, do, lse)


def lane_in_back_one(lanes, coefs, static, dxn, gain, dcoef):
    x = joined(coefs, lanes)
    r = rsqrt_mean(x)
    xr = x * r
    dgain = dxn * xr
    e = dxn * gain
    dx = r * (e - xr * (row_sum(e * xr) * (1.0 / x.shape[1])))
    for i in range(LANES):
        dcoef = dcoef + row_sum(lanes[i] * dx) * lane_mask(8 * i)
    t = coefs - static
    return dx, dgain, dcoef, dcoef * (1.0 - t * t)


def lane_in_back_two(lane, alpha, dx, dhn, r, mean):
    return alpha * dx + r * (dhn - lane * (r * mean))


def group_mean(values, lane, width):
    return row_sum(values * group_mask(lane)) * (1.0 / width)


def middle_kernel(
    info_ref,
    h_ref,
    cot_ref,
    o_ref,
    ca_ref,
    wrow_ref,
    static_ref,
    gain_ref,
    weights_ref,
    out_ref,
    dh_ref,
    dca_ref,
    do_ref,
    xb_ref,
    dgu_ref,
    hid_ref,
    dyb_ref,
    dya_ref,
    dgain_ref,
    dhyper_ref,
    dstatic_ref,
    wo,
    wgu,
    wd,
    h1,
    ya,
    yb,
    gate,
    up,
    cb,
    zb,
    rb,
    raw,
    dcoef,
    sem,
):
    rows, width = xb_ref.shape
    groups = o_ref.shape[0]
    ff = hid_ref.shape[1]
    shards = wo.shape[0]
    out_rows, gu_rows, down_rows = wo.shape[1], wgu.shape[2], wd.shape[1]
    tiles = wgu.shape[0]
    half_tiles = tiles // 2
    chunks = rows // CHUNK

    def load(start, count, where, index):
        half = shards // 2
        return [
            pltpu.make_async_copy(
                weights_ref.at[:, z, pl.ds(start, count), :],
                where.at[pl.ds(z * half, half)],
                sem.at[2 * index + z],
            )
            for z in range(2)
        ]

    copies = [load(0, out_rows, wo, 0)]
    for t in range(tiles):
        copies.append(load(out_rows + t * gu_rows, gu_rows, wgu.at[t], 1 + t))
    copies.append(load(out_rows + tiles * gu_rows, down_rows, wd, 1 + tiles))
    for pair in copies:
        for copy in pair:
            copy.start()

    def arrive(pairs):
        for pair in pairs:
            for copy in pair:
                copy.wait()

    def chunk(step):
        return pl.ds(pl.multiple_of(step * CHUNK, CHUNK), CHUNK)

    tile = 512

    def tile_at(n):
        return pl.ds(pl.multiple_of(n * tile, tile), tile)

    arrive(copies[:1])

    @pl.loop(0, width // tile)
    def _(n):
        acc = 0.0
        for j in range(groups):
            span = o_ref.shape[2]
            per = span // out_rows
            w = wo[j * per : (j + 1) * per, :, tile_at(n)].reshape(span, tile)
            acc = acc + mm(o_ref[j], w)
        ya[:, tile_at(n)] = acc

    @pl.loop(0, chunks)
    def _(step):
        rs = chunk(step)
        lanes = lanes_of(h_ref, rs, width)
        coefs = ca_ref[rs, :]
        branch = ya[rs, :]
        new = []
        for j in range(LANES):
            new.append(mixed(coefs, lanes, j) + col(coefs, 8 * j + 5) * branch)
            h1[rs, j * width : (j + 1) * width] = new[j]
        rb[rs, :] = scale_pack(new)

    acc = 0.0
    for i in range(LANES):
        cs = slice(i * width, (i + 1) * width)
        for piece in two_parts(h1[:, cs]):
            acc = acc + mm(piece, wrow_ref[i], NT)
    raw[...] = acc

    @pl.loop(0, chunks)
    def _(step):
        rs = chunk(step)
        z = fold_low(raw[rs, :]) * rb[rs, :]
        coefs = jnp.tanh(z) + static_ref[...]
        cb[rs, :] = coefs
        zb[rs, :] = z
        x = joined(coefs, lanes_of(h1, rs, width))
        xb_ref[rs, :] = (x * rsqrt_mean(x) * gain_ref[...]).astype(BF16)

    arrive(copies[1:-1])
    for t in range(half_tiles):

        @pl.loop(0, width // tile)
        def _(n):
            x = xb_ref[...]
            cs = pl.ds(pl.multiple_of(t * width + n * tile, tile), tile)
            g = mm(x, wgu[t, :, :, tile_at(n)].reshape(width, tile))
            u = mm(x, wgu[half_tiles + t, :, :, tile_at(n)].reshape(width, tile))
            gate[:, cs] = g
            up[:, cs] = u
            hid_ref[:, cs] = (g / (1.0 + jnp.exp(-g)) * u).astype(BF16)

    arrive(copies[-1:])

    @pl.loop(0, width // tile)
    def _(n):
        yb[:, tile_at(n)] = mm(hid_ref[...], wd[:, :, tile_at(n)].reshape(ff, tile))

    @pl.loop(0, chunks)
    def _(step):
        rs = chunk(step)
        per_pair = rows // 2
        pair = step * CHUNK // per_pair
        place = info_ref[2] + lax.rem(step * CHUNK, per_pair)
        spot = place + lax.broadcasted_iota(jnp.int32, (CHUNK, 1), 0)
        valid = (spot < info_ref[pair]).astype(F32)
        lanes = lanes_of(h1, rs, width)
        coefs = cb[rs, :]
        branch = yb[rs, :]
        for j in range(LANES):
            new = mixed(coefs, lanes, j) + col(coefs, 8 * j + 5) * branch
            out_ref[rs, j * width : (j + 1) * width] = new.astype(BF16)
        grads = [g * valid for g in lanes_of(cot_ref, rs, width)]
        dcoef[rs, :] = mix_grads(lanes, grads, branch)
        dyb_ref[rs, :] = branch_grad(coefs, grads).astype(BF16)

    step_ff = 2 * down_rows

    @pl.loop(0, ff // step_ff)
    def _(s):
        cs = pl.ds(pl.multiple_of(s * step_ff, 128), step_ff)
        dhid = mm(dyb_ref[...], wd[pl.ds(2 * s, 2)].reshape(step_ff, width), NT)
        g = gate[:, cs]
        z = 1.0 / (1.0 + jnp.exp(-g))
        gz = g * z
        dgu_ref[:, cs] = (dhid * up[:, cs] * (z + gz * (1.0 - z))).astype(BF16)
        cs_up = pl.ds(pl.multiple_of(ff + s * step_ff, 128), step_ff)
        dgu_ref[:, cs_up] = (dhid * gz).astype(BF16)

    per = tile // gu_rows

    @pl.loop(0, width // tile)
    def _(n):
        acc = 0.0
        for t in range(tiles):
            w = wgu[t, pl.ds(n * per, per)].reshape(tile, width)
            acc = acc + mm(dgu_ref[:, t * width : (t + 1) * width], w, NT)
        yb[:, tile_at(n)] = acc

    dgain_ref[...] = jnp.zeros_like(dgain_ref)
    dstatic_ref[...] = jnp.zeros_like(dstatic_ref)

    @pl.loop(0, chunks)
    def _(step):
        rs = chunk(step)
        lanes = lanes_of(h1, rs, width)
        dx, dgain, dc, dt = lane_in_back_one(
            lanes, cb[rs, :], static_ref[...], yb[rs, :], gain_ref[...], dcoef[rs, :]
        )
        yb[rs, :] = dx
        dgain_ref[...] += fold8(dgain)
        dstatic_ref[...] += fold8(dc)
        dcoef[rs, :] = dt

    dt_low = split_pack(dcoef[...])
    dtr_low = split_pack(dcoef[...] * rb[...])
    dh_scr = gate
    for i in range(LANES):
        cs = slice(i * width, (i + 1) * width)
        part = hyper_rows(dtr_low, h1[:, cs].astype(BF16), i)
        if i == 0:
            dhyper_ref[...] = part
        else:
            dhyper_ref[...] += part
        dhn = mm(dt_low, wrow_ref[i])
        if i < LANES - 1:
            dh_scr[:, cs] = dhn
        else:
            up[:, 0:width] = dhn

    @pl.loop(0, chunks)
    def _(step):
        rs = chunk(step)
        per_pair = rows // 2
        pair = step * CHUNK // per_pair
        place = info_ref[2] + lax.rem(step * CHUNK, per_pair)
        spot = place + lax.broadcasted_iota(jnp.int32, (CHUNK, 1), 0)
        valid = (spot < info_ref[pair]).astype(F32)
        lanes = lanes_of(h1, rs, width)
        cots = [g * valid for g in lanes_of(cot_ref, rs, width)]
        coefs = cb[rs, :]
        dx = yb[rs, :]
        dtz = dcoef[rs, :] * zb[rs, :]
        scales = rb[rs, :]
        grads = []
        for i in range(LANES):
            if i < LANES - 1:
                dhn = dh_scr[rs, i * width : (i + 1) * width]
            else:
                dhn = up[rs, 0:width]
            back = lane_in_back_two(
                lanes[i], col(coefs, 8 * i), dx, dhn, col(scales, 8 * i), group_mean(dtz, i, width)
            )
            grads.append(unmixed(coefs, cots, i) + back)
        zero = lanes_of(h_ref, rs, width)
        coefs_a = ca_ref[rs, :]
        dca_ref[rs, :] = mix_grads(zero, grads, ya[rs, :])
        dya_ref[rs, :] = branch_grad(coefs_a, grads).astype(BF16)
        for i in range(LANES):
            dh_ref[rs, i * width : (i + 1) * width] = unmixed(coefs_a, grads, i)

    @pl.loop(0, groups)
    def _(j):
        span = o_ref.shape[2]
        per = span // out_rows
        w = wo[pl.ds(j * per, per)].reshape(span, width)
        do_ref[j] = mm(dya_ref[...], w, NT).astype(BF16)


def middle(info, h, cot, o, ca, wrow, static, gain, weights, out_rows, gu_rows, down_rows):
    rows, width4 = h.shape
    width = width4 // LANES
    shards = weights.shape[0] * weights.shape[1]
    ff = shards * down_rows
    tiles = 2 * ff // width
    groups, _, span = o.shape
    vm = pl.BlockSpec(memory_space=pltpu.VMEM)
    sds = jax.ShapeDtypeStruct
    return pl.pallas_call(
        middle_kernel,
        in_specs=[pl.BlockSpec(memory_space=pltpu.SMEM)]
        + [vm] * 7
        + [pl.BlockSpec(memory_space=pl.ANY)],
        out_specs=[vm] * 12,
        out_shape=[
            sds((rows, width4), BF16),
            sds((rows, width4), F32),
            sds((rows, PACK), F32),
            sds((groups, rows, span), BF16),
            sds((rows, width), BF16),
            sds((rows, 2 * ff), BF16),
            sds((rows, ff), BF16),
            sds((rows, width), BF16),
            sds((rows, width), BF16),
            sds((8, width), F32),
            sds((8, width), F32),
            sds((8, PACK), F32),
        ],
        scratch_shapes=[
            pltpu.VMEM((shards, out_rows, width), BF16),
            pltpu.VMEM((tiles, shards, gu_rows, width), BF16),
            pltpu.VMEM((shards, down_rows, width), BF16),
            pltpu.VMEM((rows, width4), F32),
            pltpu.VMEM((rows, width), F32),
            pltpu.VMEM((rows, width), F32),
            pltpu.VMEM((rows, ff), F32),
            pltpu.VMEM((rows, ff), F32),
            pltpu.VMEM((rows, PACK), F32),
            pltpu.VMEM((rows, PACK), F32),
            pltpu.VMEM((rows, PACK), F32),
            pltpu.VMEM((rows, PACK), F32),
            pltpu.VMEM((rows, PACK), F32),
            pltpu.SemaphoreType.DMA((2 * tiles + 4,)),
        ],
        compiler_params=params(),
        name="token_local",
    )(info, h, cot, o, ca, wrow, static, gain, weights)


def turn_back_kernel(
    d_ref, u_ref, x_ref, qg_ref, kg_ref, cos_ref, sin_ref, dqkv_ref, grad_ref, dqg_ref, dkg_ref
):
    hd = qg_ref.shape[1]
    rows = x_ref.shape[0]
    half_rows = rows // 2

    @pl.when(pl.program_id(0) == 0)
    def _():
        dqg_ref[...] = jnp.zeros_like(dqg_ref)
        dkg_ref[...] = jnp.zeros_like(dkg_ref)

    for part in range(2):
        rs = slice(part * half_rows, (part + 1) * half_rows)
        cos, sin = cos_ref[...], sin_ref[...]
        for k in range(3):
            cs = slice(k * hd, (k + 1) * hd)
            u = u_ref[0, rs, cs]
            dr = d_ref[0, rs, cs].astype(F32)
            dm = dr * cos - pltpu.roll(dr, hd // 2, 1) * sin
            r = rsqrt_mean(u)
            ur = u * r
            gain = qg_ref[...] if k < 2 else kg_ref[...]
            total = dqg_ref if k < 2 else dkg_ref
            total[...] += fold8(dm * ur)
            e = dm * gain
            du = r * (e - ur * (row_sum(e * ur) * (1.0 / hd)))
            dqkv_ref[0, rs, cs] = du.astype(BF16)
        dqkv_ref[0, rs, 3 * hd :] = d_ref[0, rs, 3 * hd :]
    half = x_ref.shape[1] // 2
    for z in range(2):
        grad = mm(x_ref[:, z * half : (z + 1) * half], dqkv_ref[0], TN)
        grad_ref[:, z] = grad.astype(BF16).reshape(grad_ref.shape[0], grad_ref.shape[2], 4 * hd)


def turn_back(d, u, x, q_gain, k_gain, cos, sin, shards):
    groups, rows, width4h = d.shape
    hd = width4h // 4
    width = x.shape[1]
    sds = jax.ShapeDtypeStruct

    def whole(a):
        return pl.BlockSpec(a.shape, lambda g: (0,) * a.ndim)

    return pl.pallas_call(
        turn_back_kernel,
        grid=(groups,),
        in_specs=[
            pl.BlockSpec((1, rows, 4 * hd), lambda g: (g, 0, 0)),
            pl.BlockSpec((1, rows, 3 * hd), lambda g: (g, 0, 0)),
        ]
        + [whole(a) for a in (x, q_gain, k_gain, cos, sin)],
        out_specs=[
            pl.BlockSpec((1, rows, 4 * hd), lambda g: (g, 0, 0)),
            pl.BlockSpec((shards // 2, 2, width // shards, 4 * hd), lambda g: (0, 0, 0, g)),
            pl.BlockSpec((8, hd), lambda g: (0, 0)),
            pl.BlockSpec((8, hd), lambda g: (0, 0)),
        ],
        out_shape=[
            sds((groups, rows, 4 * hd), BF16),
            sds((shards // 2, 2, width // shards, groups * 4 * hd), BF16),
            sds((8, hd), F32),
            sds((8, hd), F32),
        ],
        compiler_params=params(),
        name="rotary_back",
    )(d, u, x, q_gain, k_gain, cos, sin)


def last_kernel(
    dqkv_ref,
    w_ref,
    h_ref,
    c_ref,
    z_ref,
    dc_ref,
    dh_ref,
    wrow_ref,
    static_ref,
    gain_ref,
    dres_ref,
    dgain_ref,
    dhyper_ref,
    dstatic_ref,
    dx_ref,
    dt_ref,
    r_ref,
):
    groups, rows, span = dqkv_ref.shape
    width = gain_ref.shape[1]
    tile = 512

    per = tile // w_ref.shape[2]
    half_tiles = width // tile // 2

    @pl.loop(0, width // tile)
    def _(n):
        z, at = n // half_tiles, lax.rem(n, half_tiles) * per
        acc = 0.0
        for g in range(groups):
            w = w_ref[pl.ds(at, per), z, :, g * span : (g + 1) * span].reshape(tile, span)
            acc = acc + mm(dqkv_ref[g], w, NT)
        dx_ref[:, pl.ds(pl.multiple_of(n * tile, tile), tile)] = acc

    dgain_ref[...] = jnp.zeros_like(dgain_ref)
    dstatic_ref[...] = jnp.zeros_like(dstatic_ref)

    def chunk(step):
        return pl.ds(pl.multiple_of(step * CHUNK, CHUNK), CHUNK)

    @pl.loop(0, rows // CHUNK)
    def _(step):
        rs = chunk(step)
        lanes = lanes_of(h_ref, rs, width)
        dx, dgain, dc, dt = lane_in_back_one(
            lanes, c_ref[rs, :], static_ref[...], dx_ref[rs, :], gain_ref[...], dc_ref[rs, :]
        )
        dx_ref[rs, :] = dx
        dgain_ref[...] += fold8(dgain)
        dstatic_ref[...] += fold8(dc)
        dt_ref[rs, :] = dt
        r_ref[rs, :] = scale_pack(lanes)

    dt_low = split_pack(dt_ref[...])
    dtr_low = split_pack(dt_ref[...] * r_ref[...])
    for i in range(LANES):
        cs = slice(i * width, (i + 1) * width)
        part = hyper_rows(dtr_low, h_ref[:, cs], i)
        if i == 0:
            dhyper_ref[...] = part
        else:
            dhyper_ref[...] += part
        dres_ref[:, cs] = mm(dt_low, wrow_ref[i])

    @pl.loop(0, rows // CHUNK)
    def _(step):
        rs = chunk(step)
        coefs = c_ref[rs, :]
        dx = dx_ref[rs, :]
        dtz = dt_ref[rs, :] * z_ref[rs, :]
        scales = r_ref[rs, :]
        for i in range(LANES):
            cs = slice(i * width, (i + 1) * width)
            lane = h_ref[rs, cs].astype(F32)
            back = lane_in_back_two(
                lane,
                col(coefs, 8 * i),
                dx,
                dres_ref[rs, cs],
                col(scales, 8 * i),
                group_mean(dtz, i, width),
            )
            dres_ref[rs, cs] = dh_ref[rs, cs] + back


def last(dqkv, w_grouped, h, c, z, dc, dh, wrow, static, gain):
    rows, width4 = h.shape
    width = width4 // LANES
    vm = pl.BlockSpec(memory_space=pltpu.VMEM)
    sds = jax.ShapeDtypeStruct
    return pl.pallas_call(
        last_kernel,
        in_specs=[vm] * 10,
        out_specs=[vm] * 4,
        out_shape=[
            sds((rows, width4), F32),
            sds((8, width), F32),
            sds((8, width), F32),
            sds((8, PACK), F32),
        ],
        scratch_shapes=[
            pltpu.VMEM((rows, width), F32),
            pltpu.VMEM((rows, PACK), F32),
            pltpu.VMEM((rows, PACK), F32),
        ],
        compiler_params=params(),
        name="lane_in_back",
    )(dqkv, w_grouped, h, c, z, dc, dh, wrow, static, gain)


def grads_kernel(o_ref, dya_ref, xb_ref, dgu_ref, hid_ref, dyb_ref, out_ref):
    per, _, owned, width = out_ref.shape
    out_rows = o_ref.shape[0] * o_ref.shape[2] // per
    gu_rows = xb_ref.shape[1] // per
    down_rows = hid_ref.shape[1] // per
    tiles = dgu_ref.shape[1] // width
    piece = mm(hid_ref[...], dyb_ref[...], TN).astype(BF16)
    for s in range(per):
        at = out_rows + tiles * gu_rows
        out_ref[s, 0, at : at + down_rows, :] = piece[s * down_rows : (s + 1) * down_rows]
    for j in range(o_ref.shape[0]):
        piece = mm(o_ref[j], dya_ref[...], TN).astype(BF16)
        heads = o_ref.shape[2] // out_rows
        for s in range(heads):
            out_ref[j * heads + s, 0, 0:out_rows, :] = piece[s * out_rows : (s + 1) * out_rows]

    for t in range(tiles):
        cs = slice(t * width, (t + 1) * width)
        piece = mm(xb_ref[...], dgu_ref[:, cs], TN).astype(BF16)
        for s in range(per):
            at = out_rows + t * gu_rows
            out_ref[s, 0, at : at + gu_rows, :] = piece[s * gu_rows : (s + 1) * gu_rows]


def weight_grads(o, dya, xb, dgu, hid, dyb, shards):
    rows, width = xb.shape
    ff = hid.shape[1]
    groups, _, span = o.shape
    steps = 4
    per = shards // steps
    owned = (groups * span + 3 * ff) // shards
    return pl.pallas_call(
        grads_kernel,
        grid=(steps,),
        in_specs=[
            pl.BlockSpec((groups // steps, rows, span), lambda g: (g, 0, 0)),
            pl.BlockSpec((rows, width), lambda g: (0, 0)),
            pl.BlockSpec((rows, width // steps), lambda g: (0, g)),
            pl.BlockSpec((rows, 2 * ff), lambda g: (0, 0)),
            pl.BlockSpec((rows, ff // steps), lambda g: (0, g)),
            pl.BlockSpec((rows, width), lambda g: (0, 0)),
        ],
        out_specs=pl.BlockSpec((per, 1, owned, width), lambda g: (g % 2, g // 2, 0, 0)),
        out_shape=jax.ShapeDtypeStruct((shards // 2, 2, owned, width), BF16),
        compiler_params=params(),
        name="weight_grads",
    )(o, dya, xb, dgu, hid, dyb)


def group_kernel(q_ref, k_ref, v_ref, out_ref, *, hd):
    groups = k_ref.shape[1] // hd
    for g in range(groups):
        at = 4 * hd * g
        out_ref[:, at : at + 2 * hd] = q_ref[:, 2 * hd * g : 2 * hd * (g + 1)]
        out_ref[:, at + 2 * hd : at + 3 * hd] = k_ref[:, hd * g : hd * (g + 1)]
        out_ref[:, at + 3 * hd : at + 4 * hd] = v_ref[:, hd * g : hd * (g + 1)]


def group_columns(q, k, v, hd):
    vm = pl.BlockSpec(memory_space=pltpu.VMEM)
    columns = q.shape[1] + k.shape[1] + v.shape[1]
    return pl.pallas_call(
        partial(group_kernel, hd=hd),
        in_specs=[vm] * 3,
        out_specs=vm,
        out_shape=jax.ShapeDtypeStruct((q.shape[0], columns), BF16),
        compiler_params=params(),
        name="group_columns",
    )(q, k, v)


def ungroup_kernel(place_ref, *refs, hd):
    pieces, (q_ref, k_ref, v_ref) = refs[:RING], refs[RING:]
    groups = k_ref.shape[1] // hd
    rows = pieces[0].shape[0]
    for d, x_ref in enumerate(pieces):
        at = pl.multiple_of(lax.rem(place_ref[0] + RING - d, RING) * rows, rows)
        rs = pl.ds(at, rows)
        for g in range(groups):
            cs = 4 * hd * g
            q_ref[rs, 2 * hd * g : 2 * hd * (g + 1)] = x_ref[:, cs : cs + 2 * hd].astype(F32)
            k_ref[rs, hd * g : hd * (g + 1)] = x_ref[:, cs + 2 * hd : cs + 3 * hd].astype(F32)
            v_ref[rs, hd * g : hd * (g + 1)] = x_ref[:, cs + 3 * hd : cs + 4 * hd].astype(F32)


def ungroup_columns(place, pieces, hd):
    vm = pl.BlockSpec(memory_space=pltpu.VMEM)
    rows, columns = pieces[0].shape
    return pl.pallas_call(
        partial(ungroup_kernel, hd=hd),
        in_specs=[pl.BlockSpec(memory_space=pltpu.SMEM)] + [vm] * RING,
        out_specs=[vm] * 3,
        out_shape=[
            jax.ShapeDtypeStruct((RING * rows, columns // part), F32) for part in (2, 4, 4)
        ],
        compiler_params=params(),
        name="ungroup_columns",
    )(place, *pieces)


def split_kernel(x_ref, out_ref, gate_ref, up_ref, down_ref):
    width = x_ref.shape[1]
    at = out_ref.shape[0]
    out_ref[...] = x_ref[0:at].astype(F32)
    for ref in (gate_ref, up_ref):
        local, ff = ref.shape
        for t in range(ff // width):
            ref[:, t * width : (t + 1) * width] = x_ref[at : at + local].astype(F32)
            at += local
    down_ref[...] = x_ref[at:].astype(F32)


def split_rows(x, out_rows, local, ff):
    vm = pl.BlockSpec(memory_space=pltpu.VMEM)
    rows, width = x.shape
    down = rows - out_rows - 2 * local * (ff // width)
    sds = jax.ShapeDtypeStruct
    return pl.pallas_call(
        split_kernel,
        in_specs=[vm],
        out_specs=[vm] * 4,
        out_shape=[
            sds((out_rows, width), F32),
            sds((local, ff), F32),
            sds((local, ff), F32),
            sds((down, width), F32),
        ],
        compiler_params=params(),
        name="split_rows",
    )(x)


RING = 4


def pair_along(kind, count, stride):
    pairs = []
    for i in range(count):
        at = i // stride % RING
        to = at ^ 1 if kind == 0 else RING - 1 - at
        pairs.append((i, i + (to - at) * stride))
    return pairs


def swap_y(values, kind):
    return lax.ppermute(values, "rep", pair_along(kind, lax.axis_size("rep"), 1))


def shift_y(values, step):
    pairs = [(r, r // RING * RING + (r + step) % RING) for r in range(lax.axis_size("rep"))]
    return lax.ppermute(values, "rep", pairs)


def swap_z(values, kind):
    rep, shard = lax.axis_size("rep"), lax.axis_size("shard")
    pairs = []
    for r in range(rep):
        for s in range(shard):
            z = 2 * (r // RING) + s // (shard // 2)
            to = z ^ 1 if kind == 0 else 3 - z
            target = (to // 2 * RING + r % RING) * shard + to % 2 * (shard // 2) + s % (shard // 2)
            pairs.append((r * shard + s, target))
    return lax.ppermute(values, ("rep", "shard"), pairs)


def z_place():
    return lax.axis_index("shard") // (lax.axis_size("shard") // 2)


def z_groups():
    half = lax.axis_size("shard") // 2
    return [list(range(half)), list(range(half, 2 * half))]


def gather_rows(block):
    mid = block.shape[1] // 2
    other = jnp.concatenate([swap_z(block[:, :mid], 0), swap_z(block[:, mid:], 1)], axis=1)
    first = z_place() == 0
    pair = jnp.stack([jnp.where(first, block, other), jnp.where(first, other, block)])
    return lax.all_gather(pair, "shard", axis_index_groups=z_groups())


def scatter_rows(parts):
    return lax.psum_scatter(
        parts, "shard", scatter_dimension=0, axis_index_groups=z_groups(), tiled=False
    )


def swap_xor(values, axis, stride):
    return lax.ppermute(values, axis, [(i, i ^ stride) for i in range(lax.axis_size(axis))])


def rep_sum(pair):
    first = z_place() == 0
    values = jnp.where(first, pair[0], pair[1])
    others = jnp.where(first, pair[1], pair[0])
    place = lax.axis_index("rep") % RING
    bits = [(place % 2 + place // 2) % 2, place // 2]
    mid = values.shape[1] // 2
    orders = ((0, 1), (1, 0))
    spans = (slice(0, mid), slice(mid, None))
    got = yield [(partial(swap_z, kind=o[0]), others[:, cs]) for o, cs in zip(orders, spans)]
    acc = [values[:, cs].astype(F32) + g.astype(F32) for cs, g in zip(spans, got)]
    half = values.shape[0]
    for step in range(2):
        half //= 2
        keep, give = [], []
        for o, a in zip(orders, acc):
            bit = bits[o[step]]
            keep.append(lax.dynamic_slice_in_dim(a, bit * half, half, 0))
            give.append(lax.dynamic_slice_in_dim(a, (1 - bit) * half, half, 0).astype(BF16))
        got = yield [(partial(swap_y, kind=o[step]), g) for o, g in zip(orders, give)]
        acc = [k + g.astype(F32) for k, g in zip(keep, got)]
    low = [a.astype(BF16) for a in acc]
    got = yield [(partial(swap_xor, axis="rep", stride=RING), v) for v in low]
    low = [(v.astype(F32) + g.astype(F32)).astype(BF16) for v, g in zip(low, got)]
    for step in (1, 0):
        got = yield [(partial(swap_y, kind=o[step]), v) for o, v in zip(orders, low)]
        for n, (o, g) in enumerate(zip(orders, got)):
            mine = bits[o[step]] == 0
            low[n] = jnp.concatenate(
                [jnp.where(mine, low[n], g), jnp.where(mine, g, low[n])], axis=0
            )
    return jnp.concatenate(low, axis=1)


def rep_sum_short(pair):
    first = z_place() == 0
    values = jnp.where(first, pair[0], pair[1])
    others = jnp.where(first, pair[1], pair[0])
    place = lax.axis_index("rep") % RING
    mid = values.shape[1] // 2
    got = yield [
        (partial(swap_z, kind=0), others[:, :mid]),
        (partial(swap_z, kind=1), others[:, mid:]),
    ]
    acc = values.astype(F32) + jnp.concatenate(got, axis=1).astype(F32)
    rows = acc.shape[0] // RING

    def quarter(d):
        return lax.dynamic_slice_in_dim(acc, (place + d) % RING * rows, rows, 0)

    shifts = range(1, RING)
    got = yield [(partial(shift_y, step=d), quarter(d).astype(BF16)) for d in shifts]
    acc = quarter(0)
    for g in got:
        acc = acc + g.astype(F32)
    low = acc.astype(BF16)
    (got,) = yield [(partial(swap_xor, axis="rep", stride=RING), low)]
    low = (low.astype(F32) + got.astype(F32)).astype(BF16)
    got = yield [(partial(shift_y, step=d), low) for d in shifts]
    return [low] + list(got)


def sum_everywhere(values):
    pairs = partial(pair_along, count=lax.axis_size("shard"), stride=2)
    swaps = [partial(swap_y, kind=0), partial(swap_y, kind=1)]
    swaps += [partial(swap_xor, axis="rep", stride=RING), partial(swap_xor, axis="shard", stride=1)]
    swaps += [lambda v, k=k: lax.ppermute(v, "shard", pairs(k)) for k in (0, 1)]
    swaps += [partial(swap_xor, axis="shard", stride=2 * RING)]
    for swap in swaps:
        (got,) = yield [(swap, values)]
        values = values + got
    return values


def rounds(*chains):
    results = [None] * len(chains)
    asked, waiting, at = {}, dict(enumerate(chains)), 0
    while asked or waiting:
        for n, (ahead, chain) in list(waiting.items()):
            if ahead <= at:
                asked[n] = next(chain)
                del waiting[n]
        got = {n: [swap(value) for swap, value in wants] for n, wants in asked.items()}
        got = lax.optimization_barrier(got)
        asked, at = {}, at + 1
        for n, values in got.items():
            try:
                asked[n] = chains[n][1].send(values)
            except StopIteration as end:
                results[n] = end.value
    return results


def rotary_tables(first, count, head_dim):
    half_dim = head_dim // 2
    inverse = ROTARY_BASE ** (-jnp.arange(half_dim, dtype=F32) * 2.0 / head_dim)
    places = (first + jnp.arange(count, dtype=jnp.int32)).astype(F32)
    angles = places[:, None] * inverse[None, :]
    cos, sin = jnp.cos(angles), jnp.sin(angles)
    return jnp.concatenate([cos, cos], axis=1), jnp.concatenate([-sin, sin], axis=1)


def packed_static(static):
    lanes, count = static.shape
    flat = jnp.pad(static, ((0, 0), (0, 8 - count))).reshape(1, lanes * 8)
    return jnp.pad(flat, ((0, 0), (0, PACK - lanes * 8)))


def on_device(
    residuals,
    lengths,
    w_query,
    w_key,
    w_value,
    w_out,
    w_gate,
    w_up,
    w_down,
    attn_gain,
    mlp_gain,
    query_gain,
    key_gain,
    hyper_weight,
    hyper_static,
    cotangent,
):
    pairs, places, lane_count, width = residuals.shape
    rows = pairs * places
    hd = query_gain.shape[0]
    rep = lax.axis_size("rep")
    shards = lax.axis_size("shard")
    local = w_query.shape[0]
    groups = w_key.shape[1] // hd
    ff = w_gate.shape[1]
    tiles = ff // width
    first = lax.axis_index("rep") * places

    grouped = group_columns(w_query, w_key, w_value, hd)
    w_grouped = gather_rows(grouped)
    rest = jnp.concatenate(
        [w_out]
        + [w_gate[:, t * width : (t + 1) * width] for t in range(tiles)]
        + [w_up[:, t * width : (t + 1) * width] for t in range(tiles)]
        + [w_down],
        axis=0,
    )
    w_rest = gather_rows(rest)

    h = residuals.reshape(rows, lane_count * width)
    cot = cotangent.reshape(rows, lane_count * width)
    wrow = pack(hyper_weight)
    wrow_a, wrow_b = wrow[0], wrow[1]
    static_a, static_b = packed_static(hyper_static[0]), packed_static(hyper_static[1])
    gain_a, gain_b = attn_gain[None, :], mlp_gain[None, :]
    q_gain, k_gain = query_gain[None, :], key_gain[None, :]
    cos, sin = rotary_tables(first, places, hd)
    info = jnp.concatenate([lengths, first[None].astype(jnp.int32)])

    xa, ca, za = pre(h, wrow_a, static_a, gain_a)
    send, keep = qkv(xa, w_grouped, q_gain, k_gain, cos, sin)
    x = lax.all_to_all(send, "rep", 0, 0, tiled=True).reshape(rep, pairs, places, 4 * hd)
    o_own, lse = attend(lengths, x)
    o = lax.all_to_all(o_own.reshape(rep, rows, 2 * hd), "rep", 0, 0, tiled=True)
    (out, dh, dca, do, xb, dgu, hid, dyb, dya, dgain_b, dhyper_b, dstatic_b) = middle(
        info,
        h,
        cot,
        o,
        ca,
        wrow_b,
        static_b,
        gain_b,
        w_rest,
        w_out.shape[0],
        local,
        w_down.shape[0],
    )
    rest_part = weight_grads(o, dya, xb, dgu, hid, dyb, shards)
    do, rest_part = lax.optimization_barrier((do, rest_part))
    do_own = lax.all_to_all(do, "rep", 0, 0, tiled=True).reshape(rep, pairs, places, 2 * hd)
    rest_own = scatter_rows(rest_part)
    d_own = attend_back(lengths, x, do_own, lse)
    d = lax.all_to_all(d_own.reshape(rep, rows, 4 * hd), "rep", 0, 0, tiled=True)
    dqkv, qkv_part, dqg, dkg = turn_back(d, keep, xa, q_gain, k_gain, cos, sin, shards)
    dres, dgain_a, dhyper_a, dstatic_a = last(
        dqkv, w_grouped, h, ca, za, dca, dh, wrow_a, static_a, gain_a
    )
    count = hyper_weight.shape[1]
    small = jnp.concatenate(
        [
            dgain_a.sum(0),
            dgain_b.sum(0),
            dqg.sum(0),
            dkg.sum(0),
            dhyper_a[:count].reshape(-1),
            dhyper_b[:count].reshape(-1),
            dstatic_a.sum(0),
            dstatic_b.sum(0),
        ]
    ).reshape(-1, PACK)
    dres, out = dres.reshape(residuals.shape), out.reshape(residuals.shape)
    qkv_part, rest_own, dres, out, small = lax.optimization_barrier(
        (qkv_part, rest_own, dres, out, small)
    )
    qkv_own = scatter_rows(qkv_part)
    rest_low, small, qkv_low = rounds(
        (0, rep_sum(rest_own)), (0, sum_everywhere(small)), (3, rep_sum_short(qkv_own))
    )
    grad_out, grad_gate, grad_up, grad_down = split_rows(rest_low, w_out.shape[0], local, ff)
    place = (lax.axis_index("rep") % RING).astype(jnp.int32)[None]
    grad_query, grad_key, grad_value = ungroup_columns(place, qkv_low, hd)
    small = small.reshape(-1)
    sizes = [width, width, hd, hd, count * width, count * width, PACK, PACK]
    pieces, start = [], 0
    for size in sizes:
        pieces.append(small[start : start + size])
        start += size

    def unpack(flat):
        return flat[: 8 * lane_count].reshape(lane_count, 8)[:, :count]

    return (
        out,
        dres,
        grad_query,
        grad_key,
        grad_value,
        grad_out,
        grad_gate,
        grad_up,
        grad_down,
        pieces[0],
        pieces[1],
        pieces[2],
        pieces[3],
        jnp.stack([pieces[4].reshape(count, width), pieces[5].reshape(count, width)]),
        jnp.stack([unpack(pieces[6]), unpack(pieces[7])]),
    )


def solution(mesh):
    lane_spec = P("shard", "rep", None, None)
    row_spec = P("shard", None)
    in_specs = (lane_spec, P("shard")) + (row_spec,) * 7 + (P(),) * 6 + (lane_spec,)
    out_specs = (lane_spec, lane_spec) + (row_spec,) * 7 + (P(),) * 6
    return jax.shard_map(
        on_device, mesh=mesh, in_specs=in_specs, out_specs=out_specs, check_vma=False
    )
```

```python
from functools import partial

import jax
import jax.numpy as jnp
from jax import lax
from jax.experimental import pallas as pl
from jax.experimental.pallas import tpu as pltpu
from jax.sharding import PartitionSpec as P

EPSILON = 1e-06
ROTARY_BASE = 1000000.0
MASKED = -1e30
LANES = 4
SPAN = 32
PACK = 128
NT = (((1,), (1,)), ((), ()))
NN = (((1,), (0,)), ((), ()))
TN = (((0,), (0,)), ((), ()))
F32 = jnp.float32
BF16 = jnp.bfloat16
VMEM_LIMIT = 60 * 1024 * 1024
CHUNK = 64


def mm(a, b, dims=NN):
    return lax.dot_general(a, b, dims, preferred_element_type=F32)


def params(limit=VMEM_LIMIT):
    return pltpu.CompilerParams(vmem_limit_bytes=limit)


def lane_mask(column):
    spot = lax.broadcasted_iota(jnp.int32, (1, PACK), 1)
    return (spot == column).astype(F32)


def group_mask(lane):
    spot = lax.broadcasted_iota(jnp.int32, (1, PACK), 1)
    return (spot // 8 == lane).astype(F32)


def row_sum(values):
    return jnp.sum(values, axis=1, keepdims=True)


def col(coefs, index):
    return coefs[:, index : index + 1]


def rsqrt_mean(values):
    return lax.rsqrt(row_sum(values * values) * (1.0 / values.shape[1]) + EPSILON)


def lanes_of(ref, rows, width):
    return [ref[rows, i * width : (i + 1) * width].astype(F32) for i in range(LANES)]


def scale_pack(lanes):
    out = 0.0
    for i, h in enumerate(lanes):
        out = out + rsqrt_mean(h) * group_mask(i)
    return out


def mixed(coefs, lanes, j):
    out = col(coefs, 1 + j) * lanes[0]
    for i in range(1, LANES):
        out = out + col(coefs, 8 * i + 1 + j) * lanes[i]
    return out


def unmixed(coefs, grads, i):
    out = col(coefs, 8 * i + 1) * grads[0]
    for j in range(1, LANES):
        out = out + col(coefs, 8 * i + 1 + j) * grads[j]
    return out


def joined(coefs, lanes):
    out = col(coefs, 0) * lanes[0]
    for i in range(1, LANES):
        out = out + col(coefs, 8 * i) * lanes[i]
    return out


def branch_grad(coefs, grads):
    out = col(coefs, 5) * grads[0]
    for j in range(1, LANES):
        out = out + col(coefs, 8 * j + 5) * grads[j]
    return out


def mix_grads(lanes, grads, branch):
    out = 0.0
    for j in range(LANES):
        for i in range(LANES):
            out = out + row_sum(lanes[i] * grads[j]) * lane_mask(8 * i + 1 + j)
        out = out + row_sum(branch * grads[j]) * lane_mask(8 * j + 5)
    return out


def fold_low(raw):
    return raw + (pltpu.roll(raw, PACK - 2 * SPAN, 1) + pltpu.roll(raw, PACK - 3 * SPAN, 1))


def two_parts(values):
    high = values.astype(BF16)
    return high, (values - high.astype(F32)).astype(BF16)


def split_pack(values):
    high = values.astype(BF16).astype(F32)
    return (high + pltpu.roll(values - high, SPAN, 1) + pltpu.roll(high, 2 * SPAN, 1)).astype(BF16)


def hyper_rows(dtr_pack, lane_low, i):
    full = mm(dtr_pack, lane_low, TN)
    return full[8 * i : 8 * i + 8] + full[SPAN + 8 * i : SPAN + 8 * i + 8]


def fold8(values):
    rows = values.shape[0]
    out = values[0:8]
    for at in range(8, rows, 8):
        out = out + values[at : at + 8]
    return out


def pack_kernel(w_ref, out_ref):
    layers, count, width = w_ref.shape
    blank = jnp.zeros((8, width), F32)
    for layer in range(layers):
        w = jnp.concatenate([w_ref[layer], jnp.zeros((8 - count, width), F32)], axis=0)
        high = w.astype(BF16).astype(F32)
        for i in range(LANES):
            pieces = [blank] * (PACK // 8)
            pieces[i] = pieces[SPAN // 8 + i] = high
            pieces[2 * SPAN // 8 + i] = low = (w - high).astype(BF16).astype(F32)
            pieces[3 * SPAN // 8 + i] = (w - high) - low
            out_ref[layer, i] = jnp.concatenate(pieces, axis=0).astype(BF16)


def pack(hyper_weight):
    layers, _, width = hyper_weight.shape
    vm = pl.BlockSpec(memory_space=pltpu.VMEM)
    return pl.pallas_call(
        pack_kernel,
        in_specs=[vm],
        out_specs=vm,
        out_shape=jax.ShapeDtypeStruct((layers, LANES, PACK, width), BF16),
        compiler_params=params(),
        name="pack_hyper_weights",
    )(hyper_weight)


def pre_kernel(h_ref, w_ref, static_ref, gain_ref, x_ref, coef_ref, z_ref, raw_ref):
    rows, width = x_ref.shape
    acc = 0.0
    for i in range(LANES):
        acc = acc + mm(h_ref[:, i * width : (i + 1) * width], w_ref[i], NT)
    raw_ref[...] = acc

    @pl.loop(0, rows // CHUNK)
    def _(step):
        rs = pl.ds(pl.multiple_of(step * CHUNK, CHUNK), CHUNK)
        lanes = lanes_of(h_ref, rs, width)
        z = fold_low(raw_ref[rs, :]) * scale_pack(lanes)
        coefs = jnp.tanh(z) + static_ref[...]
        x = joined(coefs, lanes)
        x_ref[rs, :] = (x * rsqrt_mean(x) * gain_ref[...]).astype(BF16)
        coef_ref[rs, :] = coefs
        z_ref[rs, :] = z


def pre(h, wrow, static, gain):
    rows, width4 = h.shape
    width = width4 // LANES
    block = rows // 2
    return pl.pallas_call(
        pre_kernel,
        grid=(2,),
        in_specs=[
            pl.BlockSpec((block, width4), lambda g: (g, 0)),
            pl.BlockSpec((LANES, PACK, width), lambda g: (0, 0, 0)),
            pl.BlockSpec((1, PACK), lambda g: (0, 0)),
            pl.BlockSpec((1, width), lambda g: (0, 0)),
        ],
        out_specs=[
            pl.BlockSpec((block, width), lambda g: (g, 0)),
            pl.BlockSpec((block, PACK), lambda g: (g, 0)),
            pl.BlockSpec((block, PACK), lambda g: (g, 0)),
        ],
        out_shape=[
            jax.ShapeDtypeStruct((rows, width), BF16),
            jax.ShapeDtypeStruct((rows, PACK), F32),
            jax.ShapeDtypeStruct((rows, PACK), F32),
        ],
        scratch_shapes=[pltpu.VMEM((block, PACK), F32)],
        compiler_params=params(),
        name="lane_in_zero",
    )(h, wrow, static, gain)


def rotate(u, gain, cos, sin_signed):
    half = u.shape[1] // 2
    m = u * rsqrt_mean(u) * gain
    return m * cos + pltpu.roll(m, half, 1) * sin_signed


def qkv_kernel(x_ref, w_ref, qg_ref, kg_ref, cos_ref, sin_ref, send_ref, keep_ref):
    hd = qg_ref.shape[1]
    rows = x_ref.shape[0]
    half = x_ref.shape[1] // 2
    u = 0.0
    for z in range(2):
        w = w_ref[:, z].reshape(half, 4 * hd)
        u = u + mm(x_ref[:, z * half : (z + 1) * half], w)
    half_rows = rows // 2
    for part in range(2):
        rs = slice(part * half_rows, (part + 1) * half_rows)
        cos, sin = cos_ref[...], sin_ref[...]
        for k in range(3):
            cs = slice(k * hd, (k + 1) * hd)
            piece = u[rs, cs]
            keep_ref[0, rs, cs] = piece
            gain = qg_ref[...] if k < 2 else kg_ref[...]
            send_ref[0, rs, cs] = rotate(piece, gain, cos, sin).astype(BF16)
        send_ref[0, rs, 3 * hd :] = u[rs, 3 * hd :].astype(BF16)


def qkv(x, w_grouped, q_gain, k_gain, cos, sin_signed):
    rows, width = x.shape
    hd = q_gain.shape[1]
    groups = w_grouped.shape[3] // (4 * hd)
    return pl.pallas_call(
        qkv_kernel,
        grid=(groups,),
        in_specs=[
            pl.BlockSpec((rows, width), lambda g: (0, 0)),
            pl.BlockSpec(w_grouped.shape[:3] + (4 * hd,), lambda g: (0, 0, 0, g)),
            pl.BlockSpec((1, hd), lambda g: (0, 0)),
            pl.BlockSpec((1, hd), lambda g: (0, 0)),
            pl.BlockSpec(cos.shape, lambda g: (0, 0)),
            pl.BlockSpec(cos.shape, lambda g: (0, 0)),
        ],
        out_specs=[
            pl.BlockSpec((1, rows, 4 * hd), lambda g: (g, 0, 0)),
            pl.BlockSpec((1, rows, 3 * hd), lambda g: (g, 0, 0)),
        ],
        out_shape=[
            jax.ShapeDtypeStruct((groups, rows, 4 * hd), BF16),
            jax.ShapeDtypeStruct((groups, rows, 3 * hd), F32),
        ],
        compiler_params=params(),
        name="qkv_rotary",
    )(x, w_grouped, q_gain, k_gain, cos, sin_signed)


QB = 256


def allowed_at(i, kb, length, block):
    row = lax.broadcasted_iota(jnp.int32, (2 * block, block), 0)
    row = jnp.where(row >= block, row - block, row) + i * block
    key = lax.broadcasted_iota(jnp.int32, (2 * block, block), 1) + kb * block
    return (key <= row) & (key < length)


def two_heads(ref, i, per, hd, at=0):
    first = ref[pl.ds(i * per, per), 0, :, at * hd : (at + 1) * hd]
    second = ref[pl.ds(i * per, per), 0, :, (at + 1) * hd : (at + 2) * hd]
    return jnp.concatenate([first.reshape(-1, hd), second.reshape(-1, hd)], axis=0)


def one_head(ref, i, per, hd, at):
    return ref[pl.ds(i * per, per), 0, :, at * hd : (at + 1) * hd].reshape(-1, hd)


def attend_kernel(len_ref, x_ref, o_ref, lse_ref, s_ref):
    sources, _, places, width = x_ref.shape
    hd = width // 4
    per = QB // places
    scale = hd**-0.5
    length = len_ref[pl.program_id(0)]

    @pl.loop(0, sources * places // QB)
    def _(i):
        q = two_heads(x_ref, i, per, hd)

        def score(kb, top):
            s = mm(q, one_head(x_ref, kb, per, hd, 2), NT) * scale
            s = jnp.where(allowed_at(i, kb, length, QB), s, MASKED)
            s_ref[kb] = s
            for at in range(0, QB, 128):
                top = jnp.maximum(top, s[:, at : at + 128])
            return top

        top = lax.fori_loop(0, i + 1, score, jnp.full((2 * QB, 128), MASKED, F32))
        top = jnp.max(top, axis=1, keepdims=True)

        def weigh(kb, total):
            p = jnp.exp(s_ref[kb] - top)
            s_ref[kb] = p
            for at in range(0, QB, 128):
                total = total + p[:, at : at + 128]
            return total

        total = row_sum(lax.fori_loop(0, i + 1, weigh, jnp.zeros((2 * QB, 128), F32)))
        inverse = 1.0 / total

        def gather(kb, acc):
            p = (s_ref[kb] * inverse).astype(BF16)
            return acc + mm(p, one_head(x_ref, kb, per, hd, 3))

        o = lax.fori_loop(0, i + 1, gather, jnp.zeros((2 * QB, hd), F32)).astype(BF16)
        lse_ref[0, i] = jnp.broadcast_to(top + jnp.log(total), (2 * QB, 128))
        o_ref[pl.ds(i * per, per), 0, :, 0:hd] = o[:QB].reshape(per, places, hd)
        o_ref[pl.ds(i * per, per), 0, :, hd:] = o[QB:].reshape(per, places, hd)


def attend(lengths, x):
    sources, pairs, places, width = x.shape
    hd = width // 4
    blocks = sources * places // QB
    return pl.pallas_call(
        attend_kernel,
        grid=(pairs,),
        in_specs=[
            pl.BlockSpec(memory_space=pltpu.SMEM),
            pl.BlockSpec((sources, 1, places, width), lambda b: (0, b, 0, 0)),
        ],
        out_specs=[
            pl.BlockSpec((sources, 1, places, 2 * hd), lambda b: (0, b, 0, 0)),
            pl.BlockSpec((1, blocks, 2 * QB, 128), lambda b: (b, 0, 0, 0)),
        ],
        out_shape=[
            jax.ShapeDtypeStruct((sources, pairs, places, 2 * hd), BF16),
            jax.ShapeDtypeStruct((pairs, blocks, 2 * QB, 128), F32),
        ],
        scratch_shapes=[pltpu.VMEM((blocks, 2 * QB, QB), F32)],
        compiler_params=params(),
        name="attend",
    )(lengths, x)


def attend_back_kernel(
    len_ref, x_ref, do_ref, lse_ref, out_ref, dk_ref, dv_ref, p_ref, dp_ref
):
    sources, _, places, width = x_ref.shape
    hd = width // 4
    per = QB // places
    scale = hd**-0.5
    length = len_ref[pl.program_id(0)]
    blocks = sources * places // QB
    dk_ref[...] = jnp.zeros_like(dk_ref)
    dv_ref[...] = jnp.zeros_like(dv_ref)

    @pl.loop(0, blocks)
    def _(i):
        q = two_heads(x_ref, i, per, hd)
        do = two_heads(do_ref, i, per, hd)
        lse = lse_ref[0, i][:, 0:1]

        def weigh(kb, carry):
            total, delta = carry
            s = mm(q, one_head(x_ref, kb, per, hd, 2), NT) * scale
            p = jnp.where(allowed_at(i, kb, length, QB), jnp.exp(s - lse), 0.0)
            dp = mm(do, one_head(x_ref, kb, per, hd, 3), NT)
            p_ref[kb] = p
            dp_ref[kb] = dp
            pdp = p * dp
            for at in range(0, QB, 128):
                total = total + p[:, at : at + 128]
                delta = delta + pdp[:, at : at + 128]
            dv_ref[kb] += mm(p.astype(BF16), do, TN)
            return total, delta

        zero = jnp.zeros((2 * QB, 128), F32)
        total, delta = lax.fori_loop(0, i + 1, weigh, (zero, zero))
        delta = row_sum(delta) / row_sum(total)

        def spread(kb, dq):
            ds = (p_ref[kb] * (dp_ref[kb] - delta)).astype(BF16)
            dk_ref[kb] += mm(ds, q, TN)
            return dq + mm(ds, one_head(x_ref, kb, per, hd, 2))

        dq = lax.fori_loop(0, i + 1, spread, jnp.zeros((2 * QB, hd), F32))
        dq = (dq * scale).astype(BF16)
        out_ref[pl.ds(i * per, per), 0, :, 0:hd] = dq[:QB].reshape(per, places, hd)
        out_ref[pl.ds(i * per, per), 0, :, hd : 2 * hd] = dq[QB:].reshape(per, places, hd)

    @pl.loop(0, blocks)
    def _(i):
        dk = (dk_ref[i] * scale).astype(BF16)
        out_ref[pl.ds(i * per, per), 0, :, 2 * hd : 3 * hd] = dk.reshape(per, places, hd)
        out_ref[pl.ds(i * per, per), 0, :, 3 * hd :] = (
            dv_ref[i].astype(BF16).reshape(per, places, hd)
        )


def attend_back(lengths, x, do, lse):
    sources, pairs, places, width = x.shape
    hd = width // 4
    blocks = sources * places // QB
    return pl.pallas_call(
        attend_back_kernel,
        grid=(pairs,),
        in_specs=[
            pl.BlockSpec(memory_space=pltpu.SMEM),
            pl.BlockSpec((sources, 1, places, width), lambda b: (0, b, 0, 0)),
            pl.BlockSpec((sources, 1, places, 2 * hd), lambda b: (0, b, 0, 0)),
            pl.BlockSpec((1, blocks, 2 * QB, 128), lambda b: (b, 0, 0, 0)),
        ],
        out_specs=pl.BlockSpec((sources, 1, places, width), lambda b: (0, b, 0, 0)),
        out_shape=jax.ShapeDtypeStruct((sources, pairs, places, width), BF16),
        scratch_shapes=[
            pltpu.VMEM((blocks, QB, hd), F32),
            pltpu.VMEM((blocks, QB, hd), F32),
            pltpu.VMEM((blocks, 2 * QB, QB), F32),
            pltpu.VMEM((blocks, 2 * QB, QB), F32),
        ],
        compiler_params=params(),
        name="attend_back",
    )(lengths, x, do, lse)


def lane_in_back_one(lanes, coefs, static, dxn, gain, dcoef):
    x = joined(coefs, lanes)
    r = rsqrt_mean(x)
    xr = x * r
    dgain = dxn * xr
    e = dxn * gain
    dx = r * (e - xr * (row_sum(e * xr) * (1.0 / x.shape[1])))
    for i in range(LANES):
        dcoef = dcoef + row_sum(lanes[i] * dx) * lane_mask(8 * i)
    t = coefs - static
    return dx, dgain, dcoef, dcoef * (1.0 - t * t)


def lane_in_back_two(lane, alpha, dx, dhn, r, mean):
    return alpha * dx + r * (dhn - lane * (r * mean))


def group_mean(values, lane, width):
    return row_sum(values * group_mask(lane)) * (1.0 / width)


def middle_kernel(
    info_ref,
    h_ref,
    cot_ref,
    o_ref,
    ca_ref,
    wrow_ref,
    static_ref,
    gain_ref,
    weights_ref,
    out_ref,
    dh_ref,
    dca_ref,
    do_ref,
    xb_ref,
    dgu_ref,
    hid_ref,
    dyb_ref,
    dya_ref,
    dgain_ref,
    dhyper_ref,
    dstatic_ref,
    wo,
    wgu,
    wd,
    h1,
    ya,
    yb,
    gate,
    up,
    cb,
    zb,
    rb,
    raw,
    dcoef,
    sem,
):
    rows, width = xb_ref.shape
    groups = o_ref.shape[0]
    ff = hid_ref.shape[1]
    shards = wo.shape[0]
    out_rows, gu_rows, down_rows = wo.shape[1], wgu.shape[2], wd.shape[1]
    tiles = wgu.shape[0]
    half_tiles = tiles // 2
    chunks = rows // CHUNK

    def load(start, count, where, index):
        half = shards // 2
        return [
            pltpu.make_async_copy(
                weights_ref.at[:, z, pl.ds(start, count), :],
                where.at[pl.ds(z * half, half)],
                sem.at[2 * index + z],
            )
            for z in range(2)
        ]

    copies = [load(0, out_rows, wo, 0)]
    for t in range(tiles):
        copies.append(load(out_rows + t * gu_rows, gu_rows, wgu.at[t], 1 + t))
    copies.append(load(out_rows + tiles * gu_rows, down_rows, wd, 1 + tiles))
    for pair in copies:
        for copy in pair:
            copy.start()

    def arrive(pairs):
        for pair in pairs:
            for copy in pair:
                copy.wait()

    def chunk(step):
        return pl.ds(pl.multiple_of(step * CHUNK, CHUNK), CHUNK)

    tile = 512

    def tile_at(n):
        return pl.ds(pl.multiple_of(n * tile, tile), tile)

    arrive(copies[:1])

    @pl.loop(0, width // tile)
    def _(n):
        acc = 0.0
        for j in range(groups):
            span = o_ref.shape[2]
            per = span // out_rows
            w = wo[j * per : (j + 1) * per, :, tile_at(n)].reshape(span, tile)
            acc = acc + mm(o_ref[j], w)
        ya[:, tile_at(n)] = acc

    @pl.loop(0, chunks)
    def _(step):
        rs = chunk(step)
        lanes = lanes_of(h_ref, rs, width)
        coefs = ca_ref[rs, :]
        branch = ya[rs, :]
        new = []
        for j in range(LANES):
            new.append(mixed(coefs, lanes, j) + col(coefs, 8 * j + 5) * branch)
            h1[rs, j * width : (j + 1) * width] = new[j]
        rb[rs, :] = scale_pack(new)

    acc = 0.0
    for i in range(LANES):
        cs = slice(i * width, (i + 1) * width)
        for piece in two_parts(h1[:, cs]):
            acc = acc + mm(piece, wrow_ref[i], NT)
    raw[...] = acc

    @pl.loop(0, chunks)
    def _(step):
        rs = chunk(step)
        z = fold_low(raw[rs, :]) * rb[rs, :]
        coefs = jnp.tanh(z) + static_ref[...]
        cb[rs, :] = coefs
        zb[rs, :] = z
        x = joined(coefs, lanes_of(h1, rs, width))
        xb_ref[rs, :] = (x * rsqrt_mean(x) * gain_ref[...]).astype(BF16)

    arrive(copies[1:-1])
    for t in range(half_tiles):

        @pl.loop(0, width // tile)
        def _(n):
            x = xb_ref[...]
            cs = pl.ds(pl.multiple_of(t * width + n * tile, tile), tile)
            g = mm(x, wgu[t, :, :, tile_at(n)].reshape(width, tile))
            u = mm(x, wgu[half_tiles + t, :, :, tile_at(n)].reshape(width, tile))
            gate[:, cs] = g
            up[:, cs] = u
            hid_ref[:, cs] = (g / (1.0 + jnp.exp(-g)) * u).astype(BF16)

    arrive(copies[-1:])

    @pl.loop(0, width // tile)
    def _(n):
        yb[:, tile_at(n)] = mm(hid_ref[...], wd[:, :, tile_at(n)].reshape(ff, tile))

    @pl.loop(0, chunks)
    def _(step):
        rs = chunk(step)
        per_pair = rows // 2
        pair = step * CHUNK // per_pair
        place = info_ref[2] + lax.rem(step * CHUNK, per_pair)
        spot = place + lax.broadcasted_iota(jnp.int32, (CHUNK, 1), 0)
        valid = (spot < info_ref[pair]).astype(F32)
        lanes = lanes_of(h1, rs, width)
        coefs = cb[rs, :]
        branch = yb[rs, :]
        for j in range(LANES):
            new = mixed(coefs, lanes, j) + col(coefs, 8 * j + 5) * branch
            out_ref[rs, j * width : (j + 1) * width] = new.astype(BF16)
        grads = [g * valid for g in lanes_of(cot_ref, rs, width)]
        dcoef[rs, :] = mix_grads(lanes, grads, branch)
        dyb_ref[rs, :] = branch_grad(coefs, grads).astype(BF16)

    step_ff = 2 * down_rows

    @pl.loop(0, ff // step_ff)
    def _(s):
        cs = pl.ds(pl.multiple_of(s * step_ff, 128), step_ff)
        dhid = mm(dyb_ref[...], wd[pl.ds(2 * s, 2)].reshape(step_ff, width), NT)
        g = gate[:, cs]
        z = 1.0 / (1.0 + jnp.exp(-g))
        gz = g * z
        dgu_ref[:, cs] = (dhid * up[:, cs] * (z + gz * (1.0 - z))).astype(BF16)
        cs_up = pl.ds(pl.multiple_of(ff + s * step_ff, 128), step_ff)
        dgu_ref[:, cs_up] = (dhid * gz).astype(BF16)

    per = tile // gu_rows

    @pl.loop(0, width // tile)
    def _(n):
        acc = 0.0
        for t in range(tiles):
            w = wgu[t, pl.ds(n * per, per)].reshape(tile, width)
            acc = acc + mm(dgu_ref[:, t * width : (t + 1) * width], w, NT)
        yb[:, tile_at(n)] = acc

    dgain_ref[...] = jnp.zeros_like(dgain_ref)
    dstatic_ref[...] = jnp.zeros_like(dstatic_ref)

    @pl.loop(0, chunks)
    def _(step):
        rs = chunk(step)
        lanes = lanes_of(h1, rs, width)
        dx, dgain, dc, dt = lane_in_back_one(
            lanes, cb[rs, :], static_ref[...], yb[rs, :], gain_ref[...], dcoef[rs, :]
        )
        yb[rs, :] = dx
        dgain_ref[...] += fold8(dgain)
        dstatic_ref[...] += fold8(dc)
        dcoef[rs, :] = dt

    dt_low = split_pack(dcoef[...])
    dtr_low = split_pack(dcoef[...] * rb[...])
    dh_scr = gate
    for i in range(LANES):
        cs = slice(i * width, (i + 1) * width)
        part = hyper_rows(dtr_low, h1[:, cs].astype(BF16), i)
        if i == 0:
            dhyper_ref[...] = part
        else:
            dhyper_ref[...] += part
        dhn = mm(dt_low, wrow_ref[i])
        if i < LANES - 1:
            dh_scr[:, cs] = dhn
        else:
            up[:, 0:width] = dhn

    @pl.loop(0, chunks)
    def _(step):
        rs = chunk(step)
        per_pair = rows // 2
        pair = step * CHUNK // per_pair
        place = info_ref[2] + lax.rem(step * CHUNK, per_pair)
        spot = place + lax.broadcasted_iota(jnp.int32, (CHUNK, 1), 0)
        valid = (spot < info_ref[pair]).astype(F32)
        lanes = lanes_of(h1, rs, width)
        cots = [g * valid for g in lanes_of(cot_ref, rs, width)]
        coefs = cb[rs, :]
        dx = yb[rs, :]
        dtz = dcoef[rs, :] * zb[rs, :]
        scales = rb[rs, :]
        grads = []
        for i in range(LANES):
            if i < LANES - 1:
                dhn = dh_scr[rs, i * width : (i + 1) * width]
            else:
                dhn = up[rs, 0:width]
            back = lane_in_back_two(
                lanes[i], col(coefs, 8 * i), dx, dhn, col(scales, 8 * i), group_mean(dtz, i, width)
            )
            grads.append(unmixed(coefs, cots, i) + back)
        zero = lanes_of(h_ref, rs, width)
        coefs_a = ca_ref[rs, :]
        dca_ref[rs, :] = mix_grads(zero, grads, ya[rs, :])
        dya_ref[rs, :] = branch_grad(coefs_a, grads).astype(BF16)
        for i in range(LANES):
            dh_ref[rs, i * width : (i + 1) * width] = unmixed(coefs_a, grads, i)

    @pl.loop(0, groups)
    def _(j):
        span = o_ref.shape[2]
        per = span // out_rows
        w = wo[pl.ds(j * per, per)].reshape(span, width)
        do_ref[j] = mm(dya_ref[...], w, NT).astype(BF16)


def middle(info, h, cot, o, ca, wrow, static, gain, weights, out_rows, gu_rows, down_rows):
    rows, width4 = h.shape
    width = width4 // LANES
    shards = weights.shape[0] * weights.shape[1]
    ff = shards * down_rows
    tiles = 2 * ff // width
    groups, _, span = o.shape
    vm = pl.BlockSpec(memory_space=pltpu.VMEM)
    sds = jax.ShapeDtypeStruct
    return pl.pallas_call(
        middle_kernel,
        in_specs=[pl.BlockSpec(memory_space=pltpu.SMEM)]
        + [vm] * 7
        + [pl.BlockSpec(memory_space=pl.ANY)],
        out_specs=[vm] * 12,
        out_shape=[
            sds((rows, width4), BF16),
            sds((rows, width4), F32),
            sds((rows, PACK), F32),
            sds((groups, rows, span), BF16),
            sds((rows, width), BF16),
            sds((rows, 2 * ff), BF16),
            sds((rows, ff), BF16),
            sds((rows, width), BF16),
            sds((rows, width), BF16),
            sds((8, width), F32),
            sds((8, width), F32),
            sds((8, PACK), F32),
        ],
        scratch_shapes=[
            pltpu.VMEM((shards, out_rows, width), BF16),
            pltpu.VMEM((tiles, shards, gu_rows, width), BF16),
            pltpu.VMEM((shards, down_rows, width), BF16),
            pltpu.VMEM((rows, width4), F32),
            pltpu.VMEM((rows, width), F32),
            pltpu.VMEM((rows, width), F32),
            pltpu.VMEM((rows, ff), F32),
            pltpu.VMEM((rows, ff), F32),
            pltpu.VMEM((rows, PACK), F32),
            pltpu.VMEM((rows, PACK), F32),
            pltpu.VMEM((rows, PACK), F32),
            pltpu.VMEM((rows, PACK), F32),
            pltpu.VMEM((rows, PACK), F32),
            pltpu.SemaphoreType.DMA((2 * tiles + 4,)),
        ],
        compiler_params=params(),
        name="token_local",
    )(info, h, cot, o, ca, wrow, static, gain, weights)


def turn_back_kernel(
    d_ref,
    u_ref,
    x_ref,
    qg_ref,
    kg_ref,
    cos_ref,
    sin_ref,
    o_ref,
    dya_ref,
    dqkv_ref,
    grad_ref,
    dqg_ref,
    dkg_ref,
):
    hd = qg_ref.shape[1]
    groups = o_ref.shape[0]
    step = pl.program_id(0)

    @pl.when(step == 0)
    def _():
        dqg_ref[...] = jnp.zeros_like(dqg_ref)
        dkg_ref[...] = jnp.zeros_like(dkg_ref)

    @pl.when(step < groups)
    def _():
        turn_back_group(
            d_ref, u_ref, x_ref, qg_ref, kg_ref, cos_ref, sin_ref, dqkv_ref, grad_ref, dqg_ref, dkg_ref
        )

    block, span = grad_ref.shape[2:]
    for part in range(hd // block):

        @pl.when((step - groups) // 2 == part)
        def _():
            at = pl.multiple_of(lax.rem(step, 2) * span, span)
            dya = dya_ref[:, pl.ds(at, span)]
            for g in range(groups):
                heads = [o_ref[g, :, k * hd + part * block :][:, :block] for k in range(2)]
                grad = mm(jnp.concatenate(heads, axis=1), dya, TN).astype(BF16)
                for k in range(2):
                    shard = 2 * g + k
                    grad_ref[shard % groups, shard // groups] = grad[k * block : (k + 1) * block]


def turn_back_group(
    d_ref, u_ref, x_ref, qg_ref, kg_ref, cos_ref, sin_ref, dqkv_ref, grad_ref, dqg_ref, dkg_ref
):
    hd = qg_ref.shape[1]
    rows = x_ref.shape[0]
    half_rows = rows // 2
    for part in range(2):
        rs = slice(part * half_rows, (part + 1) * half_rows)
        cos, sin = cos_ref[...], sin_ref[...]
        for k in range(3):
            cs = slice(k * hd, (k + 1) * hd)
            u = u_ref[0, rs, cs]
            dr = d_ref[0, rs, cs].astype(F32)
            dm = dr * cos - pltpu.roll(dr, hd // 2, 1) * sin
            r = rsqrt_mean(u)
            ur = u * r
            gain = qg_ref[...] if k < 2 else kg_ref[...]
            total = dqg_ref if k < 2 else dkg_ref
            total[...] += fold8(dm * ur)
            e = dm * gain
            du = r * (e - ur * (row_sum(e * ur) * (1.0 / hd)))
            dqkv_ref[0, rs, cs] = du.astype(BF16)
        dqkv_ref[0, rs, 3 * hd :] = d_ref[0, rs, 3 * hd :]
    half = x_ref.shape[1] // 2
    for z in range(2):
        grad = mm(x_ref[:, z * half : (z + 1) * half], dqkv_ref[0], TN)
        grad_ref[:, z] = grad.astype(BF16).reshape(grad_ref.shape[0], grad_ref.shape[2], 4 * hd)


def turn_back(d, u, x, q_gain, k_gain, cos, sin, o, dya, shards):
    groups, rows, width4h = d.shape
    hd = width4h // 4
    width = x.shape[1]
    block = width // shards
    per = width // (4 * hd)
    steps = groups + hd // block * per
    sds = jax.ShapeDtypeStruct

    def group(g):
        return (jnp.minimum(g, groups - 1), 0, 0)

    def whole(a):
        return pl.BlockSpec(a.shape, lambda g: (0,) * a.ndim)

    return pl.pallas_call(
        turn_back_kernel,
        grid=(steps,),
        in_specs=[
            pl.BlockSpec((1, rows, 4 * hd), group),
            pl.BlockSpec((1, rows, 3 * hd), group),
        ]
        + [whole(a) for a in (x, q_gain, k_gain, cos, sin, o, dya)],
        out_specs=[
            pl.BlockSpec((1, rows, 4 * hd), group),
            pl.BlockSpec((shards // 2, 2, block, 4 * hd), lambda g: (0, 0, g // per, g % per)),
            pl.BlockSpec((8, hd), lambda g: (0, 0)),
            pl.BlockSpec((8, hd), lambda g: (0, 0)),
        ],
        out_shape=[
            sds((groups, rows, 4 * hd), BF16),
            sds((shards // 2, 2, steps // per * block, width), BF16),
            sds((8, hd), F32),
            sds((8, hd), F32),
        ],
        compiler_params=params(),
        name="rotary_back",
    )(d, u, x, q_gain, k_gain, cos, sin, o, dya)


def last_kernel(
    dqkv_ref,
    w_ref,
    h_ref,
    c_ref,
    z_ref,
    dc_ref,
    dh_ref,
    wrow_ref,
    static_ref,
    gain_ref,
    dres_ref,
    dgain_ref,
    dhyper_ref,
    dstatic_ref,
    dx_ref,
    dt_ref,
    r_ref,
):
    groups, rows, span = dqkv_ref.shape
    width = gain_ref.shape[1]
    tile = 512

    per = tile // w_ref.shape[2]
    half_tiles = width // tile // 2

    @pl.loop(0, width // tile)
    def _(n):
        z, at = n // half_tiles, lax.rem(n, half_tiles) * per
        acc = 0.0
        for g in range(groups):
            w = w_ref[pl.ds(at, per), z, :, g * span : (g + 1) * span].reshape(tile, span)
            acc = acc + mm(dqkv_ref[g], w, NT)
        dx_ref[:, pl.ds(pl.multiple_of(n * tile, tile), tile)] = acc

    dgain_ref[...] = jnp.zeros_like(dgain_ref)
    dstatic_ref[...] = jnp.zeros_like(dstatic_ref)

    def chunk(step):
        return pl.ds(pl.multiple_of(step * CHUNK, CHUNK), CHUNK)

    @pl.loop(0, rows // CHUNK)
    def _(step):
        rs = chunk(step)
        lanes = lanes_of(h_ref, rs, width)
        dx, dgain, dc, dt = lane_in_back_one(
            lanes, c_ref[rs, :], static_ref[...], dx_ref[rs, :], gain_ref[...], dc_ref[rs, :]
        )
        dx_ref[rs, :] = dx
        dgain_ref[...] += fold8(dgain)
        dstatic_ref[...] += fold8(dc)
        dt_ref[rs, :] = dt
        r_ref[rs, :] = scale_pack(lanes)

    dt_low = split_pack(dt_ref[...])
    dtr_low = split_pack(dt_ref[...] * r_ref[...])
    for i in range(LANES):
        cs = slice(i * width, (i + 1) * width)
        part = hyper_rows(dtr_low, h_ref[:, cs], i)
        if i == 0:
            dhyper_ref[...] = part
        else:
            dhyper_ref[...] += part
        dres_ref[:, cs] = mm(dt_low, wrow_ref[i])

    @pl.loop(0, rows // CHUNK)
    def _(step):
        rs = chunk(step)
        coefs = c_ref[rs, :]
        dx = dx_ref[rs, :]
        dtz = dt_ref[rs, :] * z_ref[rs, :]
        scales = r_ref[rs, :]
        for i in range(LANES):
            cs = slice(i * width, (i + 1) * width)
            lane = h_ref[rs, cs].astype(F32)
            back = lane_in_back_two(
                lane,
                col(coefs, 8 * i),
                dx,
                dres_ref[rs, cs],
                col(scales, 8 * i),
                group_mean(dtz, i, width),
            )
            dres_ref[rs, cs] = dh_ref[rs, cs] + back


def last(dqkv, w_grouped, h, c, z, dc, dh, wrow, static, gain):
    rows, width4 = h.shape
    width = width4 // LANES
    vm = pl.BlockSpec(memory_space=pltpu.VMEM)
    sds = jax.ShapeDtypeStruct
    return pl.pallas_call(
        last_kernel,
        in_specs=[vm] * 10,
        out_specs=[vm] * 4,
        out_shape=[
            sds((rows, width4), F32),
            sds((8, width), F32),
            sds((8, width), F32),
            sds((8, PACK), F32),
        ],
        scratch_shapes=[
            pltpu.VMEM((rows, width), F32),
            pltpu.VMEM((rows, PACK), F32),
            pltpu.VMEM((rows, PACK), F32),
        ],
        compiler_params=params(),
        name="lane_in_back",
    )(dqkv, w_grouped, h, c, z, dc, dh, wrow, static, gain)


def grads_kernel(xb_ref, dgu_ref, hid_ref, dyb_ref, out_ref):
    per, _, _, width = out_ref.shape
    gu_rows = xb_ref.shape[1] // per
    down_rows = hid_ref.shape[1] // per
    tiles = dgu_ref.shape[1] // width
    piece = mm(hid_ref[...], dyb_ref[...], TN).astype(BF16)
    for s in range(per):
        out_ref[s, 0, tiles * gu_rows :, :] = piece[s * down_rows : (s + 1) * down_rows]
    for t in range(tiles):
        cs = slice(t * width, (t + 1) * width)
        piece = mm(xb_ref[...], dgu_ref[:, cs], TN).astype(BF16)
        at = t * gu_rows
        for s in range(per):
            out_ref[s, 0, at : at + gu_rows, :] = piece[s * gu_rows : (s + 1) * gu_rows]


def weight_grads(xb, dgu, hid, dyb, shards):
    rows, width = xb.shape
    ff = hid.shape[1]
    steps = 4
    per = shards // steps
    owned = 3 * ff // shards
    return pl.pallas_call(
        grads_kernel,
        grid=(steps,),
        in_specs=[
            pl.BlockSpec((rows, width // steps), lambda g: (0, g)),
            pl.BlockSpec((rows, 2 * ff), lambda g: (0, 0)),
            pl.BlockSpec((rows, ff // steps), lambda g: (0, g)),
            pl.BlockSpec((rows, width), lambda g: (0, 0)),
        ],
        out_specs=pl.BlockSpec((per, 1, owned, width), lambda g: (g % 2, g // 2, 0, 0)),
        out_shape=jax.ShapeDtypeStruct((shards // 2, 2, owned, width), BF16),
        compiler_params=params(),
        name="weight_grads",
    )(xb, dgu, hid, dyb)


def group_kernel(q_ref, k_ref, v_ref, out_ref, *, hd):
    groups = k_ref.shape[1] // hd
    for g in range(groups):
        at = 4 * hd * g
        out_ref[:, at : at + 2 * hd] = q_ref[:, 2 * hd * g : 2 * hd * (g + 1)]
        out_ref[:, at + 2 * hd : at + 3 * hd] = k_ref[:, hd * g : hd * (g + 1)]
        out_ref[:, at + 3 * hd : at + 4 * hd] = v_ref[:, hd * g : hd * (g + 1)]


def group_columns(q, k, v, hd):
    vm = pl.BlockSpec(memory_space=pltpu.VMEM)
    columns = q.shape[1] + k.shape[1] + v.shape[1]
    return pl.pallas_call(
        partial(group_kernel, hd=hd),
        in_specs=[vm] * 3,
        out_specs=vm,
        out_shape=jax.ShapeDtypeStruct((q.shape[0], columns), BF16),
        compiler_params=params(),
        name="group_columns",
    )(q, k, v)


def ungroup_kernel(place_ref, *refs, hd):
    pieces, (q_ref, k_ref, v_ref, out_ref, x_ref) = refs[:RING], refs[RING:]
    rows, width = pieces[0].shape
    local = q_ref.shape[0]
    for d, piece in enumerate(pieces):
        at = lax.rem(place_ref[0] + RING - d, RING) * rows
        x_ref[pl.ds(pl.multiple_of(at, rows), rows), :] = piece[...].astype(F32)
    per = width // (4 * hd)
    groups = k_ref.shape[1] // hd
    for g in range(groups):
        rs = slice(g // per * local, (g // per + 1) * local)
        cs = g % per * 4 * hd
        q_ref[:, 2 * hd * g : 2 * hd * (g + 1)] = x_ref[rs, cs : cs + 2 * hd]
        k_ref[:, hd * g : hd * (g + 1)] = x_ref[rs, cs + 2 * hd : cs + 3 * hd]
        v_ref[:, hd * g : hd * (g + 1)] = x_ref[rs, cs + 3 * hd : cs + 4 * hd]
    out_ref[...] = x_ref[groups // per * local :, :]


def ungroup_columns(place, pieces, hd, local, groups):
    vm = pl.BlockSpec(memory_space=pltpu.VMEM)
    rows, width = pieces[0].shape
    sds = jax.ShapeDtypeStruct
    taken = groups * 4 * hd // width * local
    return pl.pallas_call(
        partial(ungroup_kernel, hd=hd),
        in_specs=[pl.BlockSpec(memory_space=pltpu.SMEM)] + [vm] * RING,
        out_specs=[vm] * 4,
        out_shape=[
            sds((local, 2 * hd * groups), F32),
            sds((local, hd * groups), F32),
            sds((local, hd * groups), F32),
            sds((RING * rows - taken, width), F32),
        ],
        scratch_shapes=[pltpu.VMEM((RING * rows, width), F32)],
        compiler_params=params(),
        name="ungroup_columns",
    )(place, *pieces)


def small_kernel(ga_ref, gb_ref, ha_ref, hb_ref, *refs, count):
    pieces, out_ref = refs[:-1], refs[-1]
    width = out_ref.shape[1]
    mixed_row = [jnp.sum(piece[...], axis=0, keepdims=True) for piece in pieces]
    mixed_row.append(jnp.zeros((1, width - len(pieces) * PACK), F32))
    rows = [jnp.sum(ga_ref[...], axis=0, keepdims=True), jnp.sum(gb_ref[...], axis=0, keepdims=True)]
    rows += [jnp.concatenate(mixed_row, axis=1), ha_ref[:count], hb_ref[:count]]
    rows.append(jnp.zeros((out_ref.shape[0] - 3 - 2 * count, width), F32))
    out_ref[...] = jnp.concatenate(rows, axis=0)


def pack_small(gain_a, gain_b, hyper_a, hyper_b, pieces, count):
    vm = pl.BlockSpec(memory_space=pltpu.VMEM)
    return pl.pallas_call(
        partial(small_kernel, count=count),
        in_specs=[vm] * (4 + len(pieces)),
        out_specs=vm,
        out_shape=jax.ShapeDtypeStruct((16, gain_a.shape[1]), F32),
        compiler_params=params(),
        name="pack_small",
    )(gain_a, gain_b, hyper_a, hyper_b, *pieces)


def split_kernel(x_ref, gate_ref, up_ref, down_ref):
    width = x_ref.shape[1]
    at = 0
    for ref in (gate_ref, up_ref):
        local, ff = ref.shape
        for t in range(ff // width):
            ref[:, t * width : (t + 1) * width] = x_ref[at : at + local].astype(F32)
            at += local
    down_ref[...] = x_ref[at:].astype(F32)


def split_rows(x, local, ff):
    vm = pl.BlockSpec(memory_space=pltpu.VMEM)
    rows, width = x.shape
    down = rows - 2 * local * (ff // width)
    sds = jax.ShapeDtypeStruct
    return pl.pallas_call(
        split_kernel,
        in_specs=[vm],
        out_specs=[vm] * 3,
        out_shape=[sds((local, ff), F32), sds((local, ff), F32), sds((down, width), F32)],
        compiler_params=params(),
        name="split_rows",
    )(x)


RING = 4


def pair_along(kind, count, stride):
    pairs = []
    for i in range(count):
        at = i // stride % RING
        to = at ^ 1 if kind == 0 else RING - 1 - at
        pairs.append((i, i + (to - at) * stride))
    return pairs


def swap_y(values, kind):
    return lax.ppermute(values, "rep", pair_along(kind, lax.axis_size("rep"), 1))


def shift_y(values, step):
    pairs = [(r, r // RING * RING + (r + step) % RING) for r in range(lax.axis_size("rep"))]
    return lax.ppermute(values, "rep", pairs)


def swap_z(values, kind):
    rep, shard = lax.axis_size("rep"), lax.axis_size("shard")
    pairs = []
    for r in range(rep):
        for s in range(shard):
            z = 2 * (r // RING) + s // (shard // 2)
            to = z ^ 1 if kind == 0 else 3 - z
            target = (to // 2 * RING + r % RING) * shard + to % 2 * (shard // 2) + s % (shard // 2)
            pairs.append((r * shard + s, target))
    return lax.ppermute(values, ("rep", "shard"), pairs)


def z_place():
    return lax.axis_index("shard") // (lax.axis_size("shard") // 2)


def z_groups():
    half = lax.axis_size("shard") // 2
    return [list(range(half)), list(range(half, 2 * half))]


def gather_rows(block):
    mid = block.shape[1] // 2
    other = jnp.concatenate([swap_z(block[:, :mid], 0), swap_z(block[:, mid:], 1)], axis=1)
    first = z_place() == 0
    pair = jnp.stack([jnp.where(first, block, other), jnp.where(first, other, block)])
    return lax.all_gather(pair, "shard", axis_index_groups=z_groups())


def scatter_rows(parts):
    return lax.psum_scatter(
        parts, "shard", scatter_dimension=0, axis_index_groups=z_groups(), tiled=False
    )


def swap_xor(values, axis, stride):
    return lax.ppermute(values, axis, [(i, i ^ stride) for i in range(lax.axis_size(axis))])


def rep_sum(pair):
    first = z_place() == 0
    values = jnp.where(first, pair[0], pair[1])
    others = jnp.where(first, pair[1], pair[0])
    place = lax.axis_index("rep") % RING
    bits = [(place % 2 + place // 2) % 2, place // 2]
    mid = values.shape[1] // 2
    orders = ((0, 1), (1, 0))
    spans = (slice(0, mid), slice(mid, None))
    got = yield [(partial(swap_z, kind=o[0]), others[:, cs]) for o, cs in zip(orders, spans)]
    acc = [values[:, cs].astype(F32) + g.astype(F32) for cs, g in zip(spans, got)]
    half = values.shape[0]
    for step in range(2):
        half //= 2
        keep, give = [], []
        for o, a in zip(orders, acc):
            bit = bits[o[step]]
            keep.append(lax.dynamic_slice_in_dim(a, bit * half, half, 0))
            give.append(lax.dynamic_slice_in_dim(a, (1 - bit) * half, half, 0).astype(BF16))
        got = yield [(partial(swap_y, kind=o[step]), g) for o, g in zip(orders, give)]
        acc = [k + g.astype(F32) for k, g in zip(keep, got)]
    low = [a.astype(BF16) for a in acc]
    got = yield [(partial(swap_xor, axis="rep", stride=RING), v) for v in low]
    low = [(v.astype(F32) + g.astype(F32)).astype(BF16) for v, g in zip(low, got)]
    for step in (1, 0):
        got = yield [(partial(swap_y, kind=o[step]), v) for o, v in zip(orders, low)]
        for n, (o, g) in enumerate(zip(orders, got)):
            mine = bits[o[step]] == 0
            low[n] = jnp.concatenate(
                [jnp.where(mine, low[n], g), jnp.where(mine, g, low[n])], axis=0
            )
    return jnp.concatenate(low, axis=1)


def rep_sum_short(pair):
    first = z_place() == 0
    values = jnp.where(first, pair[0], pair[1])
    others = jnp.where(first, pair[1], pair[0])
    place = lax.axis_index("rep") % RING
    mid = values.shape[1] // 2
    got = yield [
        (partial(swap_z, kind=0), others[:, :mid]),
        (partial(swap_z, kind=1), others[:, mid:]),
    ]
    acc = values.astype(F32) + jnp.concatenate(got, axis=1).astype(F32)
    rows = acc.shape[0] // RING

    def quarter(d):
        return lax.dynamic_slice_in_dim(acc, (place + d) % RING * rows, rows, 0)

    shifts = range(1, RING)
    got = yield [(partial(shift_y, step=d), quarter(d).astype(BF16)) for d in shifts]
    acc = quarter(0)
    for g in got:
        acc = acc + g.astype(F32)
    low = acc.astype(BF16)
    (got,) = yield [(partial(swap_xor, axis="rep", stride=RING), low)]
    low = (low.astype(F32) + got.astype(F32)).astype(BF16)
    got = yield [(partial(shift_y, step=d), low) for d in shifts]
    return [low] + list(got)


def sum_everywhere(values):
    pairs = partial(pair_along, count=lax.axis_size("shard"), stride=2)
    swaps = [partial(swap_y, kind=0), partial(swap_y, kind=1)]
    swaps += [partial(swap_xor, axis="rep", stride=RING), partial(swap_xor, axis="shard", stride=1)]
    swaps += [lambda v, k=k: lax.ppermute(v, "shard", pairs(k)) for k in (0, 1)]
    swaps += [partial(swap_xor, axis="shard", stride=2 * RING)]
    for swap in swaps:
        (got,) = yield [(swap, values)]
        values = values + got
    return values


def rounds(beside, *chains):
    results = [None] * len(chains)
    asked, waiting, at = {}, dict(enumerate(chains)), 0
    while asked or waiting:
        for n, (ahead, chain) in list(waiting.items()):
            if ahead <= at:
                asked[n] = next(chain)
                del waiting[n]
        got = {n: [swap(value) for swap, value in wants] for n, wants in asked.items()}
        if at == 0:
            got, beside = lax.optimization_barrier((got, beside))
        else:
            got = lax.optimization_barrier(got)
        asked, at = {}, at + 1
        for n, values in got.items():
            try:
                asked[n] = chains[n][1].send(values)
            except StopIteration as end:
                results[n] = end.value
    return beside, *results


def rotary_tables(first, count, head_dim):
    half_dim = head_dim // 2
    inverse = ROTARY_BASE ** (-jnp.arange(half_dim, dtype=F32) * 2.0 / head_dim)
    places = (first + jnp.arange(count, dtype=jnp.int32)).astype(F32)
    angles = places[:, None] * inverse[None, :]
    cos, sin = jnp.cos(angles), jnp.sin(angles)
    return jnp.concatenate([cos, cos], axis=1), jnp.concatenate([-sin, sin], axis=1)


def packed_static(static):
    lanes, count = static.shape
    flat = jnp.pad(static, ((0, 0), (0, 8 - count))).reshape(1, lanes * 8)
    return jnp.pad(flat, ((0, 0), (0, PACK - lanes * 8)))


def on_device(
    residuals,
    lengths,
    w_query,
    w_key,
    w_value,
    w_out,
    w_gate,
    w_up,
    w_down,
    attn_gain,
    mlp_gain,
    query_gain,
    key_gain,
    hyper_weight,
    hyper_static,
    cotangent,
):
    pairs, places, lane_count, width = residuals.shape
    rows = pairs * places
    hd = query_gain.shape[0]
    rep = lax.axis_size("rep")
    shards = lax.axis_size("shard")
    local = w_query.shape[0]
    groups = w_key.shape[1] // hd
    ff = w_gate.shape[1]
    tiles = ff // width
    first = lax.axis_index("rep") * places

    grouped = group_columns(w_query, w_key, w_value, hd)
    w_grouped = gather_rows(grouped)
    rest = jnp.concatenate(
        [w_out]
        + [w_gate[:, t * width : (t + 1) * width] for t in range(tiles)]
        + [w_up[:, t * width : (t + 1) * width] for t in range(tiles)]
        + [w_down],
        axis=0,
    )
    w_rest = gather_rows(rest)

    h = residuals.reshape(rows, lane_count * width)
    cot = cotangent.reshape(rows, lane_count * width)
    wrow = pack(hyper_weight)
    wrow_a, wrow_b = wrow[0], wrow[1]
    static_a, static_b = packed_static(hyper_static[0]), packed_static(hyper_static[1])
    gain_a, gain_b = attn_gain[None, :], mlp_gain[None, :]
    q_gain, k_gain = query_gain[None, :], key_gain[None, :]
    cos, sin = rotary_tables(first, places, hd)
    info = jnp.concatenate([lengths, first[None].astype(jnp.int32)])

    xa, ca, za = pre(h, wrow_a, static_a, gain_a)
    send, keep = qkv(xa, w_grouped, q_gain, k_gain, cos, sin)
    x = lax.all_to_all(send, "rep", 0, 0, tiled=True).reshape(rep, pairs, places, 4 * hd)
    o_own, lse = attend(lengths, x)
    o = lax.all_to_all(o_own.reshape(rep, rows, 2 * hd), "rep", 0, 0, tiled=True)
    (out, dh, dca, do, xb, dgu, hid, dyb, dya, dgain_b, dhyper_b, dstatic_b) = middle(
        info,
        h,
        cot,
        o,
        ca,
        wrow_b,
        static_b,
        gain_b,
        w_rest,
        w_out.shape[0],
        local,
        w_down.shape[0],
    )
    rest_part = weight_grads(xb, dgu, hid, dyb, shards)
    do, rest_part = lax.optimization_barrier((do, rest_part))
    do_own = lax.all_to_all(do, "rep", 0, 0, tiled=True).reshape(rep, pairs, places, 2 * hd)
    rest_own = scatter_rows(rest_part)
    d_own = attend_back(lengths, x, do_own, lse)
    d = lax.all_to_all(d_own.reshape(rep, rows, 4 * hd), "rep", 0, 0, tiled=True)
    dqkv, qkv_part, dqg, dkg = turn_back(d, keep, xa, q_gain, k_gain, cos, sin, o, dya, shards)
    qkv_part, rest_own, dqkv = lax.optimization_barrier((qkv_part, rest_own, dqkv))
    qkv_own = scatter_rows(qkv_part)
    dres, dgain_a, dhyper_a, dstatic_a = last(
        dqkv, w_grouped, h, ca, za, dca, dh, wrow_a, static_a, gain_a
    )
    count = hyper_weight.shape[1]
    small = pack_small(
        dgain_a, dgain_b, dhyper_a, dhyper_b, (dqg, dkg, dstatic_a, dstatic_b), count
    )
    dres, out = dres.reshape(residuals.shape), out.reshape(residuals.shape)
    (dres, out), rest_low, small, qkv_low = rounds(
        (dres, out),
        (0, rep_sum(rest_own)),
        (1, sum_everywhere(small)),
        (5, rep_sum_short(qkv_own)),
    )
    grad_gate, grad_up, grad_down = split_rows(rest_low, local, ff)
    place = (lax.axis_index("rep") % RING).astype(jnp.int32)[None]
    grad_query, grad_key, grad_value, grad_out = ungroup_columns(place, qkv_low, hd, local, groups)
    pieces = [small[2, n * PACK : (n + 1) * PACK] for n in range(4)]
    top = 3 + count

    def unpack(flat):
        return flat[: 8 * lane_count].reshape(lane_count, 8)[:, :count]

    return (
        out,
        dres,
        grad_query,
        grad_key,
        grad_value,
        grad_out,
        grad_gate,
        grad_up,
        grad_down,
        small[0],
        small[1],
        pieces[0],
        pieces[1],
        jnp.stack([small[3:top], small[top : top + count]]),
        jnp.stack([unpack(pieces[2]), unpack(pieces[3])]),
    )


def solution(mesh):
    lane_spec = P("shard", "rep", None, None)
    row_spec = P("shard", None)
    in_specs = (lane_spec, P("shard")) + (row_spec,) * 7 + (P(),) * 6 + (lane_spec,)
    out_specs = (lane_spec, lane_spec) + (row_spec,) * 7 + (P(),) * 6
    return jax.shard_map(
        on_device, mesh=mesh, in_specs=in_specs, out_specs=out_specs, check_vma=False
    )
```
